32 devices in a mesh: row: 16 (over z, y, core), col: 2 (over x).
Axes of the slice: x: 2, y: 2, z: 4, core: 2. Of those that a mesh axis runs over, the one named last changes fastest.
Arguments:
- cells: bfloat16 [512, 1024, 128], P('row', 'col'), may hold values from -6 to 6
- upstream: bfloat16 [512, 1024, 128], P('row', 'col'), may hold values from -6 to 6
- counts: int32 [512], P('row'), may hold values from 1 to 1024, as said below
- key_weight: bfloat16 [128, 128], replicated, may hold values from -0.5 to 0.5
- value_weight: bfloat16 [128, 128], replicated, may hold values from -0.5 to 0.5
- out_weight: bfloat16 [128, 128], replicated, may hold values from -0.5 to 0.5
- row_query: float32 [128], replicated, may hold values from -60 to 60
- col_query: float32 [128], replicated, may hold values from -60 to 60
Outputs:
- cell_grad: bfloat16 [512, 1024, 128], P('row', 'col')
- key_weight_grad: float32 [128, 128], replicated
- value_weight_grad: float32 [128, 128], replicated
- out_weight_grad: float32 [128, 128], replicated
- row_query_grad: float32 [128], replicated
- col_query_grad: float32 [128], replicated
The draws below stay inside these ranges and needn't reach their ends.
Inputs may be any that keep to these rules, and one draw needn't show every extreme that they name: `counts`: some row uses all 1024 columns and some row uses exactly one.
All inputs are finite; a program needn't handle non-finite values.
Results may differ from the reference program's by a relative error of at most 0.0047.
Values sent between devices are 32-bit elements; how exact they have to be, the bound alone decides.
A program may use at most 192 MiB of HBM per device.

```python
import math
import jax
import jax.numpy as jnp
from jax import lax

H = 128
RD = 32
R = 512
C = 1024


def query_vector(key):
    base = jnp.clip(jax.random.normal(key, (H,), jnp.float32), -4.0, 4.0)
    return base


def draw_row_query(key, part):
    return query_vector(jax.random.fold_in(key, 11))


def draw_col_query(key, part):
    return query_vector(jax.random.fold_in(key, 23))


def draw_counts(key, part):
    key_a = jax.random.fold_in(key, 1)
    key_b = jax.random.fold_in(key, 2)
    key_c = jax.random.fold_in(key, 3)
    key_d = jax.random.fold_in(key, 4)
    first_len = jax.random.randint(key_a, (R,), 1, C + 1, jnp.int32)
    second_len = jax.random.randint(key_b, (R,), 1, C + 1, jnp.int32)
    lengths = jnp.minimum(first_len, second_len)
    full_row = jax.random.randint(key_c, (), 0, R, jnp.int32)
    short_row = (full_row + 1 + jax.random.randint(key_d, (), 0, R - 1, jnp.int32)) % R
    row_ids = jnp.arange(R, dtype=jnp.int32)
    lengths = jnp.where(row_ids == full_row, C, lengths)
    lengths = jnp.where(row_ids == short_row, 1, lengths)
    return lengths.astype(jnp.int32)


def steps_of(key, extent, cuts, least, high):
    loudness = 1.0
    for axis_at, parts in cuts:
        draws = jax.random.uniform(jax.random.fold_in(jax.random.fold_in(key, 6), axis_at), (parts,), jnp.float32, least / len(cuts), high / len(cuts))
        loudness = loudness * jnp.repeat(jnp.exp(draws), extent[axis_at] // parts).reshape((-1,) + (1,) * (len(extent) - 1 - axis_at))
    return loudness


def centred(rng, shape, spread, limit, pieces=(), held_as=jnp.bfloat16):
    level = steps_of(rng, shape, pieces, -0.22, 0.18) if pieces else 1.0
    values = jax.random.normal(rng, shape, jnp.float32) * spread * level
    return jnp.minimum(jnp.maximum(values, -limit), limit).astype(held_as)


def setup_inputs(seed: int = 0) -> dict:
    keys = jax.random.split(jax.random.key(seed), 9)
    return {
        "cells": centred(keys[0], (R, C, H), 1.0, 6.0, ((0, 16), (1, 2))),
        "upstream": centred(keys[1], (R, C, H), 1.0, 6.0, ((0, 16), (1, 2))),
        "counts": draw_counts(jax.random.fold_in(keys[8], 71), 0),
        "key_weight": centred(keys[3], (H, H), H ** -0.5, 0.5),
        "value_weight": centred(keys[4], (H, H), H ** -0.5, 0.5),
        "out_weight": centred(keys[5], (H, H), H ** -0.5, 0.5),
        "row_query": draw_row_query(jax.random.fold_in(keys[8], 71), 0),
        "col_query": draw_col_query(jax.random.fold_in(keys[8], 71), 0),
    }


NEG_FILL = -1e+30
HIGH = lax.Precision.HIGHEST

def project(block_cells, key_weight, value_weight, row_query, col_query, score_scale):
    shape = block_cells.shape
    flat_cells = block_cells.reshape(-1, shape[-1])
    key_rows = jnp.dot(flat_cells, key_weight, preferred_element_type=jnp.float32).reshape(shape)
    values = jnp.dot(flat_cells, value_weight, preferred_element_type=jnp.float32).reshape(shape)
    row_score = jnp.einsum('rch,h->rc', key_rows, row_query, precision=HIGH) * score_scale
    col_score = jnp.einsum('rch,h->rc', key_rows, col_query, precision=HIGH) * score_scale
    return (key_rows, values, row_score, col_score)

def reference(cells, upstream, counts, key_weight, value_weight, out_weight, row_query, col_query):
    score_scale = 1.0 / math.sqrt(H)
    block_count = R // RD
    cell_blocks = cells.reshape(block_count, RD, C, H)
    upstream_blocks = upstream.reshape(block_count, RD, C, H)
    count_blocks = counts.reshape(block_count, RD)
    column_ids = jnp.arange(C, dtype=jnp.int32)

    def first_pass(carry, block):
        col_max, col_total, col_pooled, col_cot = carry
        block_cells, block_up, block_counts = block
        key_rows, values, row_score, col_score = project(block_cells, key_weight, value_weight, row_query, col_query, score_scale)
        live_mask = column_ids[None, :] < block_counts[:, None]
        row_max = lax.optimization_barrier(jnp.max(jnp.where(live_mask, row_score, NEG_FILL), 1))
        row_weights = jnp.where(live_mask, jnp.exp(row_score - row_max[:, None]), 0.0)
        row_total = lax.optimization_barrier(jnp.sum(row_weights, 1))
        row_pooled = jnp.einsum('rc,rch->rh', row_weights, values, precision=HIGH)
        block_max = lax.optimization_barrier(jnp.max(jnp.where(live_mask, col_score, NEG_FILL), 0))
        joint_max = jnp.maximum(col_max, block_max)
        decay = jnp.exp(col_max - joint_max)
        col_weights = jnp.where(live_mask, jnp.exp(col_score - joint_max[None, :]), 0.0)
        col_total = col_total * decay + lax.optimization_barrier(jnp.sum(col_weights, 0))
        col_pooled = col_pooled * decay[:, None] + jnp.einsum('rc,rch->ch', col_weights, values, precision=HIGH)
        block_up_f = block_up.astype(jnp.float32)
        col_cot = col_cot + lax.optimization_barrier(jnp.sum(block_up_f, 0))
        row_cot = lax.optimization_barrier(jnp.sum(block_up_f, 1))
        return ((joint_max, col_total, col_pooled, col_cot), (row_max, row_total, row_pooled / row_total[:, None], row_cot))
    start = (jnp.full((C,), NEG_FILL, jnp.float32), jnp.zeros((C,), jnp.float32), jnp.zeros((C, H), jnp.float32), jnp.zeros((C, H), jnp.float32))
    (col_max, col_total, col_pooled, col_cot), row_parts = lax.scan(first_pass, start, (cell_blocks, upstream_blocks, count_blocks))
    col_hub = col_pooled / col_total[:, None]
    out_t = out_weight.astype(jnp.float32).T
    col_grad = jnp.dot(col_cot, out_t, precision=HIGH)
    col_dot = lax.optimization_barrier(jnp.sum(col_hub * col_grad, -1))

    def second_pass(carry, block):
        grad_key, grad_value, grad_out, grad_rq, grad_cq = carry
        block_cells, block_up, block_counts, row_max, row_total, row_hub, row_cot = block
        key_rows, values, row_score, col_score = project(block_cells, key_weight, value_weight, row_query, col_query, score_scale)
        live_mask = column_ids[None, :] < block_counts[:, None]
        row_prob = jnp.where(live_mask, jnp.exp(row_score - row_max[:, None]), 0.0) / row_total[:, None]
        col_prob = jnp.where(live_mask, jnp.exp(col_score - col_max[None, :]), 0.0) / col_total[None, :]
        row_grad = jnp.dot(row_cot, out_t, precision=HIGH)
        row_dot = lax.optimization_barrier(jnp.sum(row_hub * row_grad, -1))
        row_dp = jnp.einsum('rch,rh->rc', values, row_grad, precision=HIGH)
        col_dp = jnp.einsum('rch,ch->rc', values, col_grad, precision=HIGH)
        row_ds = row_prob * (row_dp - row_dot[:, None])
        col_ds = col_prob * (col_dp - col_dot[None, :])
        value_grad = (row_prob[..., None] * row_grad[:, None, :] + col_prob[..., None] * col_grad[None, :, :]).astype(jnp.bfloat16)
        key_grad = ((row_ds[..., None] * row_query + col_ds[..., None] * col_query) * score_scale).astype(jnp.bfloat16)
        grad_rq = grad_rq + jnp.einsum('rc,rch->h', row_ds, key_rows, precision=HIGH) * score_scale
        grad_cq = grad_cq + jnp.einsum('rc,rch->h', col_ds, key_rows, precision=HIGH) * score_scale
        flat_cells = block_cells.reshape(-1, H)
        flat_kg = key_grad.reshape(-1, H)
        flat_vg = value_grad.reshape(-1, H)
        grad_key = grad_key + jnp.einsum('nh,nk->hk', flat_cells, flat_kg, preferred_element_type=jnp.float32)
        grad_value = grad_value + jnp.einsum('nh,nk->hk', flat_cells, flat_vg, preferred_element_type=jnp.float32)
        grad_out = grad_out + jnp.einsum('rh,rk->hk', row_hub, row_cot, precision=HIGH)
        back = jnp.einsum('nk,hk->nh', flat_kg, key_weight, preferred_element_type=jnp.float32)
        back = back + jnp.einsum('nk,hk->nh', flat_vg, value_weight, preferred_element_type=jnp.float32)
        cell_block = (block_up.astype(jnp.float32) + back.reshape(block_up.shape)).astype(jnp.bfloat16)
        return ((grad_key, grad_value, grad_out, grad_rq, grad_cq), cell_block)
    zero_mat = jnp.zeros((H, H), jnp.float32)
    zero_vec = jnp.zeros((H,), jnp.float32)
    row_max, row_total, row_hub, row_cot = row_parts
    (grad_key, grad_value, grad_out, grad_rq, grad_cq), cell_blocks_out = lax.scan(second_pass, (zero_mat, zero_mat, zero_mat, zero_vec, zero_vec), (cell_blocks, upstream_blocks, count_blocks, row_max, row_total, row_hub, row_cot))
    grad_out = grad_out + jnp.einsum('ch,ck->hk', col_hub, col_cot, precision=HIGH)
    return (cell_blocks_out.reshape(R, C, H), grad_key, grad_value, grad_out, grad_rq, grad_cq)
```

```python
import functools
import math

import jax
import jax.numpy as jnp
from jax import lax
from jax.experimental import pallas as pl
from jax.experimental.pallas import tpu as pltpu
from jax.sharding import PartitionSpec as P

NEG_FILL = -1e30
HIGH = lax.Precision.HIGHEST
MESH = pl.DeviceIdType.MESH
F32 = jnp.float32
BF16 = jnp.bfloat16
VMEM_BYTES = 48 * 1024 * 1024


def dot_nt(a, b, precision=None):
    return lax.dot_general(
        a, b, (((1,), (1,)), ((), ())), precision=precision, preferred_element_type=F32
    )


def dot_tn(a, b, precision=None):
    return lax.dot_general(
        a, b, (((0,), (0,)), ((), ())), precision=precision, preferred_element_type=F32
    )


def split(x, parts):
    pieces = []
    for _ in range(parts):
        piece = x.astype(BF16).astype(F32)
        pieces.append(piece)
        x = x - piece
    return pieces


def stack_rows(rows, width):
    pad = jnp.zeros((16 - len(rows), width), F32)
    return jnp.concatenate(rows + [pad], 0).astype(BF16)


def flat_row(tile):
    return jnp.concatenate([tile[i : i + 1] for i in range(tile.shape[0])], 1)


def stats_kernel(
    n_row, n_col, chunk,
    cells_hbm, up_hbm, counts, wk_ref, wv_ref, wo_ref, rq_ref, cq_ref,
    lhs_out, base_out, g_out, kwg_out, vwg_out, owg_out, qg_out,
    cells, up, cot_loc, rs_buf, cot_full, row_cot, sr, sc, wr, wc, rdp, cdp,
    row_pool, row_grad, col_pool, row_buf, small, red_src, red_buf, part, m_full,
    cell_sem, up_sem, s_rs, r_rs, s_ag, r_ag, s_rx, r_rx, s_sm, r_sm, s_rd, r_rd,
    s_cx, r_cx, s_mg, r_mg,
):
    rows, cols, width = cells.shape
    scale = 1.0 / math.sqrt(width)
    me_r = lax.axis_index("row")
    me_c = lax.axis_index("col")
    n_chunk = rows // chunk
    per = cols // n_row
    m_per = width // n_row
    q_rows = cols // 128

    def local(hbm, vmem, sem, k):
        return pltpu.make_async_copy(
            hbm.at[pl.ds(k * chunk, chunk)], vmem.at[pl.ds(k * chunk, chunk)], sem.at[k]
        )

    for k in range(n_chunk):
        local(up_hbm, up, up_sem, k).start()
    for k in range(n_chunk):
        local(cells_hbm, cells, cell_sem, k).start()

    barrier = pltpu.get_barrier_semaphore()

    @pl.loop(1, n_row)
    def _(d):
        pl.semaphore_signal(
            barrier, inc=1, device_id=(lax.rem(me_r + d, n_row), me_c), device_id_type=MESH
        )

    @pl.loop(1, n_col)
    def _(d):
        pl.semaphore_signal(
            barrier, inc=1, device_id=(me_r, lax.rem(me_c + d, n_col)), device_id_type=MESH
        )

    def to_rows(src_of, dst, s_sem, r_sem, d):
        peer = lax.rem(me_r + d, n_row)
        return pltpu.make_async_remote_copy(
            src_ref=src_of(peer), dst_ref=dst.at[me_r], send_sem=s_sem.at[d],
            recv_sem=r_sem.at[d], device_id=(peer, me_c), device_id_type=MESH,
        )

    def from_rows(src_of, dst, s_sem, r_sem, d):
        peer = lax.rem(me_r + n_row - d, n_row)
        return pltpu.make_async_remote_copy(
            src_ref=src_of(peer), dst_ref=dst.at[peer], send_sem=s_sem.at[d],
            recv_sem=r_sem.at[d], device_id=(peer, me_c), device_id_type=MESH,
        )

    def to_cols(src, dst, s_sem, r_sem, d):
        peer = lax.rem(me_c + d, n_col)
        return pltpu.make_async_remote_copy(
            src_ref=src, dst_ref=dst.at[me_c], send_sem=s_sem.at[d],
            recv_sem=r_sem.at[d], device_id=(me_r, peer), device_id_type=MESH,
        )

    def from_cols(src, dst, s_sem, r_sem, d):
        peer = lax.rem(me_c + n_col - d, n_col)
        return pltpu.make_async_remote_copy(
            src_ref=src, dst_ref=dst.at[peer], send_sem=s_sem.at[d],
            recv_sem=r_sem.at[d], device_id=(me_r, peer), device_id_type=MESH,
        )

    def start_rows(*args):
        @pl.loop(1, n_row)
        def _(d):
            to_rows(*args, d).start()

    def wait_rows(*args):
        @pl.loop(1, n_row)
        def _(d):
            to_rows(*args, d).wait_send()
            from_rows(*args, d).wait_recv()

    def start_cols(*args):
        @pl.loop(1, n_col)
        def _(d):
            to_cols(*args, d).start()

    def wait_cols(*args):
        @pl.loop(1, n_col)
        def _(d):
            to_cols(*args, d).wait_send()
            from_cols(*args, d).wait_recv()

    span = 64
    groups = span // per
    for k in range(n_chunk):
        local(up_hbm, up, up_sem, k).wait()

        def add_block(cb, total, k=k):
            x = up[pl.ds(k * chunk, chunk), pl.ds(pl.multiple_of(cb * span, span), span), :]
            x = x.astype(F32)
            by_col = jnp.sum(x, 0).reshape(groups, per, width)
            at = pl.ds(cb * groups, groups)
            cot_loc[at] = by_col if k == 0 else cot_loc[at] + by_col
            return total + jnp.sum(x, 1)

        row_cot[pl.ds(k * chunk, chunk), :] = lax.fori_loop(
            0, cols // span, add_block, jnp.zeros((chunk, width), F32)
        )

    pl.semaphore_wait(barrier, n_row + n_col - 2)
    scatter = (lambda peer: cot_loc.at[peer], rs_buf, s_rs, r_rs)
    start_rows(*scatter)
    rs_buf[me_r] = cot_loc[me_r]

    wk = wk_ref[...].astype(F32)
    queries = jnp.concatenate([rq_ref[...], cq_ref[...], jnp.zeros((6, width), F32)], 0)
    kvec = dot_nt(queries, wk, HIGH) * scale
    kr, kc = kvec[0:1], kvec[1:2]
    k_pieces = stack_rows(split(kr, 3) + split(kc, 3), width)
    ids = me_c * cols + lax.broadcasted_iota(jnp.int32, (1, cols), 1)
    for k in range(n_chunk):
        local(cells_hbm, cells, cell_sem, k).wait()

        @pl.loop(k * chunk, (k + 1) * chunk)
        def _(r):
            s = dot_nt(k_pieces, cells[r])
            live = ids < counts[r]
            sr[pl.ds(r, 1), :] = jnp.where(live, s[0:1] + s[1:2] + s[2:3], NEG_FILL)
            sc[pl.ds(r, 1), :] = jnp.where(live, s[3:4] + s[4:5] + s[5:6], NEG_FILL)

    wait_rows(*scatter)
    own = rs_buf[0]
    for i in range(1, n_row):
        own = own + rs_buf[i]
    cot_full[me_r] = own
    gather = (lambda peer: cot_full.at[me_r], cot_full, s_ag, r_ag)
    start_rows(*gather)

    score = sr[...]
    row_m = jnp.max(score, 1, keepdims=True)
    weight = jnp.where(score > 0.5 * NEG_FILL, jnp.exp(score - row_m), 0.0)
    wr[...] = weight
    row_t = jnp.sum(weight, 1, keepdims=True)

    @pl.loop(0, rows)
    def _(r):
        pieces = stack_rows(split(wr[pl.ds(r, 1), :], 2), cols)
        s = jnp.dot(pieces, cells[r], preferred_element_type=F32)
        row_pool[pl.ds(r, 1), :] = s[0:1] + s[1:2]

    row_buf[me_c, 0] = row_pool[...]
    row_buf[me_c, 1] = row_cot[...]
    row_buf[me_c, 2] = jnp.broadcast_to(row_m, (rows, width))
    row_buf[me_c, 3] = jnp.broadcast_to(row_t, (rows, width))
    row_x = (row_buf.at[me_c], row_buf, s_rx, r_rx)
    start_cols(*row_x)

    score = sc[...]
    col_m = jnp.max(score, 0, keepdims=True)
    weight = jnp.where(score > 0.5 * NEG_FILL, jnp.exp(score - col_m), 0.0)
    wc[...] = weight
    col_t = jnp.sum(weight, 0, keepdims=True)
    w_t = jnp.concatenate([p.T for p in split(weight, 2)], 1).astype(BF16)
    pick = lax.rem(lax.broadcasted_iota(jnp.int32, (2 * rows, width), 0), rows)
    col_pool[...] = jnp.zeros_like(col_pool)

    @pl.loop(0, rows)
    def _(r):
        one = jnp.where(pick == r, 1.0, 0.0).astype(BF16)
        spread = jnp.dot(w_t, one, preferred_element_type=F32)
        col_pool[...] += spread * cells[r].astype(F32)

    wait_cols(*row_x)
    top = row_buf[0, 2]
    for i in range(1, n_col):
        top = jnp.maximum(top, row_buf[i, 2])
    pool = jnp.zeros((rows, width), F32)
    total = jnp.zeros((rows, width), F32)
    cot = jnp.zeros((rows, width), F32)
    for i in range(n_col):
        decay = jnp.exp(row_buf[i, 2] - top)
        pool = pool + row_buf[i, 0] * decay
        total = total + row_buf[i, 3] * decay
        cot = cot + row_buf[i, 1]
    factor = jnp.exp(row_buf[me_c, 2] - top) / total
    both = jnp.dot(wv_ref[...], wo_ref[...], preferred_element_type=F32)
    g_row = dot_nt(cot, both, HIGH)
    row_grad[...] = g_row
    row_dot = jnp.sum(pool * g_row, 1, keepdims=True) / total[:, 0:1]
    row_prob = wr[...] * factor[:, 0:1]

    @pl.loop(0, rows)
    def _(r):
        s = dot_nt(stack_rows(split(row_grad[pl.ds(r, 1), :], 3), width), cells[r])
        rdp[pl.ds(r, 1), :] = s[0:1] + s[1:2] + s[2:3]

    wait_rows(*gather)
    cot_all = cot_full[...].reshape(cols, width)
    g_col = dot_nt(cot_all, both, HIGH)
    g_out[...] = g_col
    ones = jnp.ones((16, width), BF16)

    @pl.loop(0, rows)
    def _(r):
        prod = cells[r].astype(F32) * g_out[...]
        hi = prod.astype(BF16)
        lo = (prod - hi.astype(F32)).astype(BF16)
        s = dot_nt(ones, hi) + dot_nt(ones, lo)
        cdp[pl.ds(r, 1), :] = s[0:1]

    part_dot = jnp.sum(wc[...] * cdp[...], 0, keepdims=True)
    for j, value in enumerate((col_m, col_t, part_dot)):
        for i in range(q_rows):
            small[me_r, pl.ds(j * q_rows + i, 1), :] = value[:, i * 128 : (i + 1) * 128]
    small_x = (lambda peer: small.at[me_r], small, s_sm, r_sm)
    start_rows(*small_x)
    row_ds = row_prob * (rdp[...] - row_dot)
    wait_rows(*small_x)
    top = small[0, 0:q_rows]
    for i in range(1, n_row):
        top = jnp.maximum(top, small[i, 0:q_rows])
    total = jnp.zeros((q_rows, 128), F32)
    dots = jnp.zeros((q_rows, 128), F32)
    for i in range(n_row):
        decay = jnp.exp(small[i, 0:q_rows] - top)
        total = total + small[i, q_rows : 2 * q_rows] * decay
        dots = dots + small[i, 2 * q_rows : 3 * q_rows] * decay
    f_col = jnp.exp(col_m - flat_row(top)) / flat_row(total)
    col_prob = wc[...] * f_col
    col_ds = col_prob * (cdp[...] - flat_row(dots / total))

    sr[...] = row_ds
    sc[...] = col_ds

    def moments(r, acc):
        pieces = split(sr[pl.ds(r, 1), :], 2) + split(sc[pl.ds(r, 1), :], 2)
        return acc + jnp.dot(stack_rows(pieces, cols), cells[r], preferred_element_type=F32)

    acc = lax.fori_loop(0, rows, moments, jnp.zeros((16, width), F32))
    f_t = jnp.broadcast_to(f_col, (8, cols)).T[:, 0:1]
    m_loc = dot_tn(col_pool[...] * f_t, cot_all, HIGH)
    m_loc = m_loc + dot_tn(row_pool[...] * factor, cot, HIGH)
    ab = jnp.concatenate([acc[0:1] + acc[1:2], acc[2:3] + acc[3:4], jnp.zeros((6, width), F32)], 0)
    for i in range(n_row):
        red_src[i, 0:m_per] = m_loc[i * m_per : (i + 1) * m_per]
        if m_per < 8:
            red_src[i, m_per:8] = jnp.zeros((8 - m_per, width), F32)
        red_src[i, 8:16] = ab
    reduce = (lambda peer: red_src.at[peer], red_buf, s_rd, r_rd)
    start_rows(*reduce)
    red_buf[me_r] = red_src[me_r]

    groups4 = (row_prob, row_ds, col_ds, col_prob)
    pieces = [split(x, 2) for x in groups4]
    for half in range(2):
        block = jnp.concatenate([p[half] for p in pieces], 0)
        lhs_out[:, half * 4 * rows : (half + 1) * 4 * rows] = block.T.astype(BF16)
    zero = jnp.zeros((rows, width), F32)
    one = jnp.ones((rows, width), F32)
    left = jnp.concatenate(
        [g_row, jnp.broadcast_to(kr, (rows, width)), jnp.broadcast_to(kc, (rows, width)), zero], 0
    )
    right = jnp.concatenate([zero, zero, zero, one], 0)
    half = jnp.concatenate([left, right], 1)
    base_out[...] = jnp.concatenate([half, half], 0)

    wait_rows(*reduce)
    acc = red_buf[0]
    for i in range(1, n_row):
        acc = acc + red_buf[i]
    part[me_c] = acc
    col_x = (part.at[me_c], part, s_cx, r_cx)
    start_cols(*col_x)
    wait_cols(*col_x)
    acc = part[0]
    for i in range(1, n_col):
        acc = acc + part[i]
    m_full[me_r] = acc[0:8]
    collect = (lambda peer: m_full.at[me_r], m_full, s_mg, r_mg)
    start_rows(*collect)
    ab = acc[8:16]
    kwg_out[...] = dot_tn(ab, queries * scale, HIGH)
    qg_out[...] = jnp.dot(ab, wk, precision=HIGH, preferred_element_type=F32) * scale
    wait_rows(*collect)
    m = jnp.concatenate([m_full[i, 0:m_per] for i in range(n_row)], 0)
    vwg_out[...] = dot_nt(m, wo_ref[...].astype(F32), HIGH)
    owg_out[...] = dot_tn(wv_ref[...].astype(F32), m, HIGH)


def cell_kernel(rows, lhs_ref, base_ref, g_ref, up_ref, out_ref):
    block = up_ref.shape[0]
    width = up_ref.shape[2]
    step = pl.program_id(0)
    owner = lax.rem(lax.broadcasted_iota(jnp.int32, base_ref.shape, 0), rows)

    @pl.loop(0, block)
    def _(i):
        rhs = jnp.where(owner == step * block + i, base_ref[...], 0.0).astype(BF16)
        res = jnp.dot(lhs_ref[...], rhs, preferred_element_type=F32)
        delta = res[:, :width] + res[:, width:] * g_ref[...]
        out_ref[i] = (up_ref[i].astype(F32) + delta).astype(out_ref.dtype)


def on_device(n_row, n_col, cells, upstream, counts, wk, wv, wo, rq, cq):
    rows, cols, width = cells.shape
    chunk = 8
    per = cols // n_row
    vmem = pl.BlockSpec(memory_space=pltpu.VMEM)
    hbm = pl.BlockSpec(memory_space=pl.ANY)
    n_chunk = rows // chunk
    dma = pltpu.SemaphoreType.DMA
    f32 = lambda *shape: pltpu.VMEM(shape, F32)
    small_rows = -(-3 * (cols // 128) // 8) * 8
    square = jax.ShapeDtypeStruct((width, width), F32)
    lhs, base, g_col, kwg, vwg, owg, qg = pl.pallas_call(
        functools.partial(stats_kernel, n_row, n_col, chunk),
        out_shape=(
            jax.ShapeDtypeStruct((cols, 8 * rows), BF16),
            jax.ShapeDtypeStruct((8 * rows, 2 * width), F32),
            jax.ShapeDtypeStruct((cols, width), F32),
            square, square, square,
            jax.ShapeDtypeStruct((8, width), F32),
        ),
        in_specs=[hbm, hbm, pl.BlockSpec(memory_space=pltpu.SMEM)] + [vmem] * 5,
        out_specs=(vmem,) * 7,
        scratch_shapes=[
            pltpu.VMEM(cells.shape, BF16), pltpu.VMEM(cells.shape, BF16),
            f32(n_row, per, width), f32(n_row, per, width), f32(n_row, per, width),
            f32(rows, width),
            f32(rows, cols), f32(rows, cols), f32(rows, cols), f32(rows, cols),
            f32(rows, cols), f32(rows, cols),
            f32(rows, width), f32(rows, width), f32(cols, width),
            f32(n_col, 4, rows, width),
            f32(n_row, small_rows, 128),
            f32(n_row, 16, width), f32(n_row, 16, width), f32(n_col, 16, width),
            f32(n_row, 8, width),
            dma((n_chunk,)), dma((n_chunk,)),
            dma((n_row,)), dma((n_row,)), dma((n_row,)), dma((n_row,)),
            dma((n_col,)), dma((n_col,)), dma((n_row,)), dma((n_row,)),
            dma((n_row,)), dma((n_row,)), dma((n_col,)), dma((n_col,)),
            dma((n_row,)), dma((n_row,)),
        ],
        compiler_params=pltpu.CompilerParams(
            collective_id=0, has_side_effects=True, vmem_limit_bytes=VMEM_BYTES
        ),
        name="hub_stats",
    )(cells, upstream, counts, wk, wv, wo, rq.reshape(1, width), cq.reshape(1, width))
    block = 4
    whole = lambda shape: pl.BlockSpec(shape, lambda i: (0,) * len(shape))
    cell_spec = pl.BlockSpec((block, cols, width), lambda i: (i, 0, 0))
    cell_grad = pl.pallas_call(
        functools.partial(cell_kernel, rows),
        grid=(rows // block,),
        out_shape=jax.ShapeDtypeStruct(cells.shape, cells.dtype),
        in_specs=[whole(lhs.shape), whole(base.shape), whole(g_col.shape), cell_spec],
        out_specs=cell_spec,
        compiler_params=pltpu.CompilerParams(vmem_limit_bytes=VMEM_BYTES),
        name="cell_grad",
    )(lhs, base, g_col, upstream)
    return cell_grad, kwg, vwg, owg, qg[0], qg[1]


def solution(mesh):
    placed = (P("row", "col", None), P("row", "col", None), P("row"), P(), P(), P(), P(), P())
    return jax.shard_map(
        functools.partial(on_device, mesh.shape["row"], mesh.shape["col"]),
        mesh=mesh,
        in_specs=placed,
        out_specs=(P("row", "col", None), P(), P(), P(), P(), P()),
        check_vma=False,
    )
```

```python
import functools
import math

import jax
import jax.numpy as jnp
from jax import lax
from jax.experimental import pallas as pl
from jax.experimental.pallas import tpu as pltpu
from jax.sharding import PartitionSpec as P

NEG_FILL = -1e30
HIGH = lax.Precision.HIGHEST
MESH = pl.DeviceIdType.MESH
F32 = jnp.float32
BF16 = jnp.bfloat16
VMEM_BYTES = 62 * 1024 * 1024


def dot_nt(a, b, precision=None):
    return lax.dot_general(
        a, b, (((1,), (1,)), ((), ())), precision=precision, preferred_element_type=F32
    )


def dot_tn(a, b, precision=None):
    return lax.dot_general(
        a, b, (((0,), (0,)), ((), ())), precision=precision, preferred_element_type=F32
    )


def dot_nn(a, b, precision=None):
    return jnp.dot(a, b, precision=precision, preferred_element_type=F32)


def split(x, parts):
    pieces = []
    for _ in range(parts):
        piece = x.astype(BF16).astype(F32)
        pieces.append(piece)
        x = x - piece
    return pieces


def stack_rows(rows, width):
    pad = jnp.zeros((16 - len(rows), width), F32)
    return jnp.concatenate(rows + [pad], 0).astype(BF16)


def flat_row(tile):
    return jnp.concatenate([tile[i : i + 1] for i in range(tile.shape[0])], 1)


def stats_kernel(
    n_row, n_col, chunk,
    cells_hbm, up_hbm, counts, wk_hbm, wv_hbm, wo_hbm, rq_hbm, cq_hbm,
    lhs_out, base_out, g_out, m_out, ab_out,
    cells, up, cot_loc, rs_buf, cot_full, row_cot, sr, sc, wr, wc, rdp, cdp,
    row_pool, row_grad, col_pool, row_buf, small, dots_buf, red_src, red_buf, part, m_full,
    ab_buf, ab_part, wk_ref, wv_ref, wo_ref, rq_ref, cq_ref,
    cell_sem, up_sem, in_sem, s_rs, r_rs, s_ag, r_ag, s_rx, r_rx, s_sm, r_sm, s_dt, r_dt,
    s_rd, r_rd, s_cx, r_cx, s_mg, r_mg, s_ab, r_ab, s_ac, r_ac,
):
    rows, cols, width = cells.shape
    scale = 1.0 / math.sqrt(width)
    me_r = lax.axis_index("row")
    me_c = lax.axis_index("col")
    n_chunk = rows // chunk
    per = cols // n_row
    m_per = width // n_row
    q_rows = cols // 128

    def local(hbm, vmem, sem, k):
        return pltpu.make_async_copy(
            hbm.at[pl.ds(k * chunk, chunk)], vmem.at[pl.ds(k * chunk, chunk)], sem.at[k]
        )

    for k in range(n_chunk):
        local(up_hbm, up, up_sem, k).start()
    small_in = [
        pltpu.make_async_copy(src, dst, in_sem.at[i])
        for i, (src, dst) in enumerate(
            ((wk_hbm, wk_ref), (wv_hbm, wv_ref), (wo_hbm, wo_ref), (rq_hbm, rq_ref), (cq_hbm, cq_ref))
        )
    ]
    for copy in small_in:
        copy.start()
    for k in range(n_chunk):
        local(cells_hbm, cells, cell_sem, k).start()
    sub16 = lax.broadcasted_iota(jnp.int32, (16, width), 0)

    barrier = pltpu.get_barrier_semaphore()

    @pl.loop(1, n_row)
    def _(d):
        pl.semaphore_signal(
            barrier, inc=1, device_id=(lax.rem(me_r + d, n_row), me_c), device_id_type=MESH
        )

    @pl.loop(1, n_col)
    def _(d):
        pl.semaphore_signal(
            barrier, inc=1, device_id=(me_r, lax.rem(me_c + d, n_col)), device_id_type=MESH
        )

    def to_rows(src_of, dst, s_sem, r_sem, d):
        peer = lax.rem(me_r + d, n_row)
        return pltpu.make_async_remote_copy(
            src_ref=src_of(peer), dst_ref=dst.at[me_r], send_sem=s_sem.at[d],
            recv_sem=r_sem.at[d], device_id=(peer, me_c), device_id_type=MESH,
        )

    def from_rows(src_of, dst, s_sem, r_sem, d):
        peer = lax.rem(me_r + n_row - d, n_row)
        return pltpu.make_async_remote_copy(
            src_ref=src_of(peer), dst_ref=dst.at[peer], send_sem=s_sem.at[d],
            recv_sem=r_sem.at[d], device_id=(peer, me_c), device_id_type=MESH,
        )

    def to_cols(src, dst, s_sem, r_sem, d):
        peer = lax.rem(me_c + d, n_col)
        return pltpu.make_async_remote_copy(
            src_ref=src, dst_ref=dst.at[me_c], send_sem=s_sem.at[d],
            recv_sem=r_sem.at[d], device_id=(me_r, peer), device_id_type=MESH,
        )

    def from_cols(src, dst, s_sem, r_sem, d):
        peer = lax.rem(me_c + n_col - d, n_col)
        return pltpu.make_async_remote_copy(
            src_ref=src, dst_ref=dst.at[peer], send_sem=s_sem.at[d],
            recv_sem=r_sem.at[d], device_id=(me_r, peer), device_id_type=MESH,
        )

    def start_rows(*args):
        @pl.loop(1, n_row)
        def _(d):
            to_rows(*args, d).start()

    def wait_rows(*args):
        @pl.loop(1, n_row)
        def _(d):
            to_rows(*args, d).wait_send()
            from_rows(*args, d).wait_recv()

    def start_cols(*args):
        @pl.loop(1, n_col)
        def _(d):
            to_cols(*args, d).start()

    def wait_cols(*args):
        @pl.loop(1, n_col)
        def _(d):
            to_cols(*args, d).wait_send()
            from_cols(*args, d).wait_recv()

    span = 64
    groups = span // per
    for k in range(n_chunk):
        local(up_hbm, up, up_sem, k).wait()

        def add_block(cb, total, k=k):
            x = up[pl.ds(k * chunk, chunk), pl.ds(pl.multiple_of(cb * span, span), span), :]
            x = x.astype(F32)
            by_col = jnp.sum(x, 0).reshape(groups, per, width)
            at = pl.ds(cb * groups, groups)
            cot_loc[at] = by_col if k == 0 else cot_loc[at] + by_col
            return total + jnp.sum(x, 1)

        row_cot[pl.ds(k * chunk, chunk), :] = lax.fori_loop(
            0, cols // span, add_block, jnp.zeros((chunk, width), F32)
        )

    pl.semaphore_wait(barrier, n_row + n_col - 2)
    scatter = (lambda peer: cot_loc.at[peer], rs_buf, s_rs, r_rs)
    start_rows(*scatter)
    rs_buf[me_r] = cot_loc[me_r]

    for copy in small_in:
        copy.wait()
    wk = wk_ref[...].astype(F32)
    queries = jnp.concatenate([rq_ref[...], cq_ref[...], jnp.zeros((6, width), F32)], 0)
    kvec = dot_nt(queries, wk, HIGH) * scale
    kr, kc = kvec[0:1], kvec[1:2]
    k_pieces = stack_rows(split(kr, 3) + split(kc, 3), width)
    ids = me_c * cols + lax.broadcasted_iota(jnp.int32, (1, cols), 1)

    @pl.loop(0, n_chunk)
    def _(k):
        local(cells_hbm, cells, cell_sem, k).wait()
        at = pl.ds(pl.multiple_of(k * chunk, chunk), chunk)
        s = dot_nt(k_pieces, cells[at].reshape(chunk * cols, width))
        one, two = [], []
        for i in range(chunk):
            x = s[:, i * cols : (i + 1) * cols]
            live = ids < counts[k * chunk + i]
            one.append(jnp.where(live, x[0:1] + x[1:2] + x[2:3], NEG_FILL))
            two.append(jnp.where(live, x[3:4] + x[4:5] + x[5:6], NEG_FILL))
        sr[at, :] = jnp.concatenate(one, 0)
        sc[at, :] = jnp.concatenate(two, 0)

    wait_rows(*scatter)
    own = rs_buf[0]
    for i in range(1, n_row):
        own = own + rs_buf[i]
    cot_full[me_r] = own
    gather = (lambda peer: cot_full.at[me_r], cot_full, s_ag, r_ag)
    start_rows(*gather)

    score = sc[...]
    col_m = jnp.max(score, 0, keepdims=True)
    weight = jnp.where(score > 0.5 * NEG_FILL, jnp.exp(score - col_m), 0.0)
    wc[...] = weight
    col_t = jnp.sum(weight, 0, keepdims=True)
    for j, value in enumerate((col_m, col_t)):
        for i in range(q_rows):
            small[me_r, pl.ds(j * q_rows + i, 1), :] = value[:, i * 128 : (i + 1) * 128]
    small_x = (lambda peer: small.at[me_r], small, s_sm, r_sm)
    start_rows(*small_x)

    score = sr[...]
    row_m = jnp.max(score, 1, keepdims=True)
    row_weight = jnp.where(score > 0.5 * NEG_FILL, jnp.exp(score - row_m), 0.0)
    wr[...] = row_weight
    row_t = jnp.sum(row_weight, 1, keepdims=True)
    sub = lax.broadcasted_iota(jnp.int32, (chunk, 1), 0)

    @pl.loop(0, n_chunk)
    def _(k):
        at = pl.ds(pl.multiple_of(k * chunk, chunk), chunk)
        pieces = jnp.concatenate(split(wr[at, :], 2), 0).astype(BF16)
        acc = jnp.zeros((chunk, width), F32)
        for i in range(chunk):
            s = jnp.dot(pieces, cells[k * chunk + i], preferred_element_type=F32)
            acc = jnp.where(sub == i, s[0:chunk] + s[chunk : 2 * chunk], acc)
        row_pool[at, :] = acc

    row_buf[me_c, 0] = row_pool[...]
    row_buf[me_c, 1] = row_cot[...]
    row_buf[me_c, 2] = jnp.broadcast_to(row_m, (rows, width))
    row_buf[me_c, 3] = jnp.broadcast_to(row_t, (rows, width))
    row_x = (row_buf.at[me_c], row_buf, s_rx, r_rx)
    start_cols(*row_x)

    w_t = jnp.concatenate([p.T for p in split(weight, 2)], 1).astype(BF16)
    pick = lax.rem(lax.broadcasted_iota(jnp.int32, (2 * rows, 2 * width), 0), rows)
    lane = lax.broadcasted_iota(jnp.int32, (2 * rows, 2 * width), 1)
    pick = pick - jnp.where(lane < width, 0, 1)
    col_pool[...] = jnp.zeros_like(col_pool)

    @pl.loop(0, rows // 4)
    def _(k):
        acc = col_pool[...]
        for i in (0, 2):
            r = k * 4 + i
            one = jnp.where(pick == r, 1.0, 0.0).astype(BF16)
            spread = jnp.dot(w_t, one, preferred_element_type=F32)
            acc = acc + spread[:, :width] * cells[r].astype(F32)
            acc = acc + spread[:, width:] * cells[r + 1].astype(F32)
        col_pool[...] = acc

    wait_cols(*row_x)
    top = row_buf[0, 2]
    for i in range(1, n_col):
        top = jnp.maximum(top, row_buf[i, 2])
    pool = jnp.zeros((rows, width), F32)
    total = jnp.zeros((rows, width), F32)
    cot = jnp.zeros((rows, width), F32)
    for i in range(n_col):
        decay = jnp.exp(row_buf[i, 2] - top)
        pool = pool + row_buf[i, 0] * decay
        total = total + row_buf[i, 3] * decay
        cot = cot + row_buf[i, 1]
    factor = jnp.exp(row_buf[me_c, 2] - top) / total
    both = jnp.dot(wv_ref[...], wo_ref[...], preferred_element_type=F32)
    g_row = dot_nt(cot, both, HIGH)
    row_grad[...] = g_row
    row_dot = jnp.sum(pool * g_row, 1, keepdims=True) / total[:, 0:1]
    row_prob = wr[...] * factor[:, 0:1]

    @pl.loop(0, n_chunk)
    def _(k):
        at = pl.ds(pl.multiple_of(k * chunk, chunk), chunk)
        pieces = jnp.concatenate(split(row_grad[at, :], 2), 0).astype(BF16)
        acc = jnp.zeros((chunk, cols), F32)
        for i in range(chunk):
            s = dot_nt(pieces, cells[k * chunk + i])
            acc = jnp.where(sub == i, s[0:chunk] + s[chunk : 2 * chunk], acc)
        rdp[at, :] = acc

    row_ds = row_prob * (rdp[...] - row_dot)
    sr[...] = row_ds

    wait_rows(*small_x)
    top = small[0, 0:q_rows]
    for i in range(1, n_row):
        top = jnp.maximum(top, small[i, 0:q_rows])
    total = jnp.zeros((q_rows, 128), F32)
    for i in range(n_row):
        total = total + small[i, q_rows : 2 * q_rows] * jnp.exp(small[i, 0:q_rows] - top)
    f_col = jnp.exp(col_m - flat_row(top)) / flat_row(total)
    col_prob = wc[...] * f_col
    wc[...] = col_prob
    f_t = jnp.broadcast_to(f_col, (8, cols)).T[:, 0:1]

    wait_rows(*gather)
    cot_all = cot_full[...].reshape(cols, width)
    m_loc = dot_tn(col_pool[...] * f_t, cot_all, HIGH)
    m_loc = m_loc + dot_tn(row_pool[...] * factor, cot, HIGH)
    for i in range(n_row):
        red_src[i, 0:m_per] = m_loc[i * m_per : (i + 1) * m_per]
        if m_per < 8:
            red_src[i, m_per:8] = jnp.zeros((8 - m_per, width), F32)
    reduce = (lambda peer: red_src.at[peer], red_buf, s_rd, r_rd)
    start_rows(*reduce)
    red_buf[me_r] = red_src[me_r]

    g_col = dot_nt(cot_all, both, HIGH)
    g_out[...] = g_col

    @pl.loop(0, n_chunk)
    def _(k):
        at = pl.ds(pl.multiple_of(k * chunk, chunk), chunk)
        acc = jnp.zeros((16, cols), F32)
        for i in range(chunk):
            prod = cells[k * chunk + i].astype(F32) * g_out[...]
            hi = prod.astype(BF16)
            lo = (prod - hi.astype(F32)).astype(BF16)
            ones = jnp.where(sub16 == i, 1.0, 0.0).astype(BF16)
            acc = acc + dot_nt(ones, hi) + dot_nt(ones, lo)
        cdp[at, :] = acc[0:chunk]

    part_dot = jnp.sum(wc[...] * cdp[...], 0, keepdims=True)
    for i in range(q_rows):
        dots_buf[me_r, pl.ds(i, 1), :] = part_dot[:, i * 128 : (i + 1) * 128]
    dots_x = (lambda peer: dots_buf.at[me_r], dots_buf, s_dt, r_dt)
    start_rows(*dots_x)

    wait_rows(*reduce)
    acc = red_buf[0]
    for i in range(1, n_row):
        acc = acc + red_buf[i]
    part[me_c] = acc
    col_x = (part.at[me_c], part, s_cx, r_cx)
    start_cols(*col_x)

    wait_rows(*dots_x)
    dots = dots_buf[0, 0:q_rows]
    for i in range(1, n_row):
        dots = dots + dots_buf[i, 0:q_rows]
    col_ds = wc[...] * (cdp[...] - flat_row(dots))
    sc[...] = col_ds

    turn = lax.rem(lax.broadcasted_iota(jnp.int32, (4 * chunk, 1), 0), chunk)

    def moments(k, acc):
        at = pl.ds(pl.multiple_of(k * chunk, chunk), chunk)
        pieces = split(sr[at, :], 2) + split(sc[at, :], 2)
        pieces = jnp.concatenate(pieces, 0).astype(BF16)
        for i in range(chunk):
            s = jnp.dot(pieces, cells[k * chunk + i], preferred_element_type=F32)
            acc = acc + jnp.where(turn == i, s, 0.0)
        return acc

    acc = lax.fori_loop(0, n_chunk, moments, jnp.zeros((4 * chunk, width), F32))
    ab_buf[me_r] = jnp.concatenate(
        [
            jnp.sum(acc[0 : 2 * chunk], 0, keepdims=True),
            jnp.sum(acc[2 * chunk : 4 * chunk], 0, keepdims=True),
            jnp.zeros((6, width), F32),
        ],
        0,
    )
    ab_x = (lambda peer: ab_buf.at[me_r], ab_buf, s_ab, r_ab)
    start_rows(*ab_x)

    wait_cols(*col_x)
    acc = part[0]
    for i in range(1, n_col):
        acc = acc + part[i]
    m_full[me_r] = acc
    collect = (lambda peer: m_full.at[me_r], m_full, s_mg, r_mg)
    start_rows(*collect)

    pieces = [split(x, 2) for x in (row_prob, row_ds, col_ds, wc[...])]
    for half in range(2):
        block = jnp.concatenate([p[half] for p in pieces], 0)
        lhs_out[:, half * 4 * rows : (half + 1) * 4 * rows] = block.T.astype(BF16)
    zero = jnp.zeros((rows, width), F32)
    one = jnp.ones((rows, width), F32)
    left = jnp.concatenate(
        [g_row, jnp.broadcast_to(kr, (rows, width)), jnp.broadcast_to(kc, (rows, width)), zero], 0
    )
    right = jnp.concatenate([zero, zero, zero, one], 0)
    half = jnp.concatenate([left, right], 1)
    base_out[...] = jnp.concatenate([half, half], 0)

    wait_rows(*ab_x)
    acc = ab_buf[0]
    for i in range(1, n_row):
        acc = acc + ab_buf[i]
    ab_part[me_c] = acc
    ab_cx = (ab_part.at[me_c], ab_part, s_ac, r_ac)
    start_cols(*ab_cx)
    wait_rows(*collect)
    m_out[...] = jnp.concatenate([m_full[i, 0:m_per] for i in range(n_row)], 0)
    wait_cols(*ab_cx)
    acc = ab_part[0]
    for i in range(1, n_col):
        acc = acc + ab_part[i]
    ab_out[...] = acc


def cell_kernel(
    rows, lhs_ref, base_ref, g_ref, m_ref, ab_ref, wk_ref, wv_ref, wo_ref, rq_ref, cq_ref, up_ref,
    out_ref, kwg_ref, vwg_ref, owg_ref, rqg_ref, cqg_ref,
):
    block = up_ref.shape[0]
    width = up_ref.shape[2]
    step = pl.program_id(0)
    scale = 1.0 / math.sqrt(width)
    owner = lax.rem(lax.broadcasted_iota(jnp.int32, base_ref.shape, 0), rows)

    @pl.when(step == 0)
    def _():
        ab, m = ab_ref[...], m_ref[...]
        queries = jnp.concatenate([rq_ref[...], cq_ref[...], jnp.zeros((6, width), F32)], 0)
        kwg_ref[...] = dot_tn(ab, queries * scale, HIGH)
        q_grad = dot_nn(ab, wk_ref[...].astype(F32), HIGH) * scale
        rqg_ref[...] = q_grad[0:1]
        cqg_ref[...] = q_grad[1:2]
        vwg_ref[...] = dot_nt(m, wo_ref[...].astype(F32), HIGH)
        owg_ref[...] = dot_tn(wv_ref[...].astype(F32), m, HIGH)

    @pl.loop(0, block, unroll=4)
    def _(i):
        rhs = jnp.where(owner == step * block + i, base_ref[...], 0.0).astype(BF16)
        res = jnp.dot(lhs_ref[...], rhs, preferred_element_type=F32)
        delta = res[:, :width] + res[:, width:] * g_ref[...]
        out_ref[i] = (up_ref[i].astype(F32) + delta).astype(out_ref.dtype)


def on_device(n_row, n_col, cells, upstream, counts, wk, wv, wo, rq, cq):
    rows, cols, width = cells.shape
    chunk = 8
    per = cols // n_row
    rq, cq = rq.reshape(1, width), cq.reshape(1, width)
    vmem = pl.BlockSpec(memory_space=pltpu.VMEM)
    hbm = pl.BlockSpec(memory_space=pl.ANY)
    n_chunk = rows // chunk
    dma = pltpu.SemaphoreType.DMA
    f32 = lambda *shape: pltpu.VMEM(shape, F32)
    small_rows = -(-2 * (cols // 128) // 8) * 8
    dots_rows = -(-(cols // 128) // 8) * 8
    square = jax.ShapeDtypeStruct((width, width), F32)
    vector = jax.ShapeDtypeStruct((1, width), F32)
    over_row, over_col = dma((n_row,)), dma((n_col,))
    lhs, base, g_col, m, ab = pl.pallas_call(
        functools.partial(stats_kernel, n_row, n_col, chunk),
        out_shape=(
            jax.ShapeDtypeStruct((cols, 8 * rows), BF16),
            jax.ShapeDtypeStruct((8 * rows, 2 * width), F32),
            jax.ShapeDtypeStruct((cols, width), F32),
            square,
            jax.ShapeDtypeStruct((8, width), F32),
        ),
        in_specs=[hbm, hbm, pl.BlockSpec(memory_space=pltpu.SMEM)] + [hbm] * 5,
        out_specs=(vmem,) * 5,
        scratch_shapes=[
            pltpu.VMEM(cells.shape, BF16), pltpu.VMEM(cells.shape, BF16),
            f32(n_row, per, width), f32(n_row, per, width), f32(n_row, per, width),
            f32(rows, width),
            f32(rows, cols), f32(rows, cols), f32(rows, cols), f32(rows, cols),
            f32(rows, cols), f32(rows, cols),
            f32(rows, width), f32(rows, width), f32(cols, width),
            f32(n_col, 4, rows, width),
            f32(n_row, small_rows, 128), f32(n_row, dots_rows, 128),
            f32(n_row, 8, width), f32(n_row, 8, width), f32(n_col, 8, width),
            f32(n_row, 8, width),
            f32(n_row, 8, width), f32(n_col, 8, width),
            pltpu.VMEM(wk.shape, BF16), pltpu.VMEM(wv.shape, BF16), pltpu.VMEM(wo.shape, BF16),
            f32(1, width), f32(1, width),
            dma((n_chunk,)), dma((n_chunk,)), dma((5,)),
            over_row, over_row, over_row, over_row,
            over_col, over_col, over_row, over_row, over_row, over_row,
            over_row, over_row, over_col, over_col, over_row, over_row,
            over_row, over_row, over_col, over_col,
        ],
        compiler_params=pltpu.CompilerParams(
            collective_id=0, has_side_effects=True, vmem_limit_bytes=VMEM_BYTES
        ),
        name="hub_stats",
    )(cells, upstream, counts, wk, wv, wo, rq, cq)
    block = 8
    whole = lambda shape: pl.BlockSpec(shape, lambda i: (0,) * len(shape))
    cell_spec = pl.BlockSpec((block, cols, width), lambda i: (i, 0, 0))
    fixed = (lhs, base, g_col, m, ab, wk, wv, wo, rq, cq)
    cell_grad, kwg, vwg, owg, rqg, cqg = pl.pallas_call(
        functools.partial(cell_kernel, rows),
        grid=(rows // block,),
        out_shape=(
            jax.ShapeDtypeStruct(cells.shape, cells.dtype),
            square, square, square, vector, vector,
        ),
        in_specs=[whole(x.shape) for x in fixed] + [cell_spec],
        out_specs=(cell_spec,) + (whole((width, width)),) * 3 + (whole((1, width)),) * 2,
        compiler_params=pltpu.CompilerParams(vmem_limit_bytes=VMEM_BYTES),
        name="cell_grad",
    )(*fixed, upstream)
    return cell_grad, kwg, vwg, owg, rqg.reshape(width), cqg.reshape(width)


def solution(mesh):
    placed = (P("row", "col", None), P("row", "col", None), P("row"), P(), P(), P(), P(), P())
    return jax.shard_map(
        functools.partial(on_device, mesh.shape["row"], mesh.shape["col"]),
        mesh=mesh,
        in_specs=placed,
        out_specs=(P("row", "col", None), P(), P(), P(), P(), P()),
        check_vma=False,
    )
```

```python
import functools
import math

import jax
import jax.numpy as jnp
from jax import lax
from jax.experimental import pallas as pl
from jax.experimental.pallas import tpu as pltpu
from jax.sharding import PartitionSpec as P

NEG_FILL = -1e30
HIGH = lax.Precision.HIGHEST
MESH = pl.DeviceIdType.MESH
F32 = jnp.float32
BF16 = jnp.bfloat16
VMEM_BYTES = 62 * 1024 * 1024


def dot_nt(a, b, precision=None):
    return lax.dot_general(
        a, b, (((1,), (1,)), ((), ())), precision=precision, preferred_element_type=F32
    )


def dot_tn(a, b, precision=None):
    return lax.dot_general(
        a, b, (((0,), (0,)), ((), ())), precision=precision, preferred_element_type=F32
    )


def dot_nn(a, b, precision=None):
    return jnp.dot(a, b, precision=precision, preferred_element_type=F32)


def split(x, parts):
    pieces = []
    for _ in range(parts):
        piece = x.astype(BF16).astype(F32)
        pieces.append(piece)
        x = x - piece
    return pieces


def stack_rows(rows, width):
    pad = jnp.zeros((16 - len(rows), width), F32)
    return jnp.concatenate(rows + [pad], 0).astype(BF16)


def flat_row(tile):
    return jnp.concatenate([tile[i : i + 1] for i in range(tile.shape[0])], 1)


def stats_kernel(
    n_row, n_col, chunk,
    cells_hbm, up_hbm, counts, wk_hbm, wv_hbm, wo_hbm, rq_hbm, cq_hbm,
    lhs_out, base_out, g_out, m_out, ab_out,
    cells, up, cot_loc, pair_buf, chip_sum, rs_buf, cot_full, row_cot, sr, sc, wr, wc, rdp, cdp,
    row_pool, row_grad, col_pool, row_buf, small, dots_buf, red_src, red_buf, part, m_full,
    ab_buf, ab_part, wk_ref, wv_ref, wo_ref, rq_ref, cq_ref,
    cell_sem, up_sem, in_sem, s_pr, r_pr, s_rs, r_rs, s_ag, r_ag, s_rx, r_rx, s_sm, r_sm, s_dt, r_dt,
    s_rd, r_rd, s_cx, r_cx, s_mg, r_mg, s_ab, r_ab, s_ac, r_ac,
):
    rows, cols, width = cells.shape
    scale = 1.0 / math.sqrt(width)
    me_r = lax.axis_index("row")
    me_c = lax.axis_index("col")
    n_chunk = rows // chunk
    per = cols // n_row
    m_per = width // n_row
    q_rows = cols // 128

    def local(hbm, vmem, sem, k):
        return pltpu.make_async_copy(
            hbm.at[pl.ds(k * chunk, chunk)], vmem.at[pl.ds(k * chunk, chunk)], sem.at[k]
        )

    for k in range(n_chunk):
        local(up_hbm, up, up_sem, k).start()
    small_in = [
        pltpu.make_async_copy(src, dst, in_sem.at[i])
        for i, (src, dst) in enumerate(
            ((wk_hbm, wk_ref), (wv_hbm, wv_ref), (wo_hbm, wo_ref), (rq_hbm, rq_ref), (cq_hbm, cq_ref))
        )
    ]
    for copy in small_in:
        copy.start()
    for k in range(n_chunk):
        local(cells_hbm, cells, cell_sem, k).start()
    sub16 = lax.broadcasted_iota(jnp.int32, (16, width), 0)

    barrier = pltpu.get_barrier_semaphore()

    @pl.loop(1, n_row)
    def _(d):
        pl.semaphore_signal(
            barrier, inc=1, device_id=(lax.rem(me_r + d, n_row), me_c), device_id_type=MESH
        )

    @pl.loop(1, n_col)
    def _(d):
        pl.semaphore_signal(
            barrier, inc=1, device_id=(me_r, lax.rem(me_c + d, n_col)), device_id_type=MESH
        )

    def to_rows(src_of, dst, s_sem, r_sem, d):
        peer = lax.rem(me_r + d, n_row)
        return pltpu.make_async_remote_copy(
            src_ref=src_of(peer), dst_ref=dst.at[me_r], send_sem=s_sem.at[d],
            recv_sem=r_sem.at[d], device_id=(peer, me_c), device_id_type=MESH,
        )

    def from_rows(src_of, dst, s_sem, r_sem, d):
        peer = lax.rem(me_r + n_row - d, n_row)
        return pltpu.make_async_remote_copy(
            src_ref=src_of(peer), dst_ref=dst.at[peer], send_sem=s_sem.at[d],
            recv_sem=r_sem.at[d], device_id=(peer, me_c), device_id_type=MESH,
        )

    def to_cols(src, dst, s_sem, r_sem, d):
        peer = lax.rem(me_c + d, n_col)
        return pltpu.make_async_remote_copy(
            src_ref=src, dst_ref=dst.at[me_c], send_sem=s_sem.at[d],
            recv_sem=r_sem.at[d], device_id=(me_r, peer), device_id_type=MESH,
        )

    def from_cols(src, dst, s_sem, r_sem, d):
        peer = lax.rem(me_c + n_col - d, n_col)
        return pltpu.make_async_remote_copy(
            src_ref=src, dst_ref=dst.at[peer], send_sem=s_sem.at[d],
            recv_sem=r_sem.at[d], device_id=(me_r, peer), device_id_type=MESH,
        )

    half_n = n_row // 2
    me_core, me_chip = lax.rem(me_r, 2), lax.div(me_r, 2)
    mine, other = me_core * half_n, (1 - me_core) * half_n

    def to_sibling(src, dst, s_sem, r_sem):
        return pltpu.make_async_remote_copy(
            src_ref=src, dst_ref=dst, send_sem=s_sem, recv_sem=r_sem,
            device_id=(me_r + 1 - 2 * me_core, me_c), device_id_type=MESH,
        )

    def to_chips(src_of, dst, s_sem, r_sem, d):
        chip = lax.rem(me_chip + d, half_n)
        return pltpu.make_async_remote_copy(
            src_ref=src_of(chip), dst_ref=dst, send_sem=s_sem.at[d], recv_sem=r_sem.at[d],
            device_id=(chip * 2 + me_core, me_c), device_id_type=MESH,
        )

    def from_chips(dst_of, s_sem, r_sem, d):
        chip = lax.rem(me_chip + half_n - d, half_n)
        return pltpu.make_async_remote_copy(
            src_ref=dst_of(chip), dst_ref=dst_of(chip), send_sem=s_sem.at[d],
            recv_sem=r_sem.at[d], device_id=(chip * 2 + me_core, me_c), device_id_type=MESH,
        )

    def start_rows(*args):
        @pl.loop(1, n_row)
        def _(d):
            to_rows(*args, d).start()

    def wait_rows(*args):
        @pl.loop(1, n_row)
        def _(d):
            to_rows(*args, d).wait_send()
            from_rows(*args, d).wait_recv()

    def start_cols(*args):
        @pl.loop(1, n_col)
        def _(d):
            to_cols(*args, d).start()

    def wait_cols(*args):
        @pl.loop(1, n_col)
        def _(d):
            to_cols(*args, d).wait_send()
            from_cols(*args, d).wait_recv()

    span = 64
    groups = span // per
    for k in range(n_chunk):
        local(up_hbm, up, up_sem, k).wait()

        def add_block(cb, total, k=k):
            x = up[pl.ds(k * chunk, chunk), pl.ds(pl.multiple_of(cb * span, span), span), :]
            x = x.astype(F32)
            by_col = jnp.sum(x, 0).reshape(groups, per, width)
            at = pl.ds(cb * groups, groups)
            cot_loc[at] = by_col if k == 0 else cot_loc[at] + by_col
            return total + jnp.sum(x, 1)

        row_cot[pl.ds(k * chunk, chunk), :] = lax.fori_loop(
            0, cols // span, add_block, jnp.zeros((chunk, width), F32)
        )

    pl.semaphore_wait(barrier, n_row + n_col - 2)
    swap = to_sibling(cot_loc.at[pl.ds(other, half_n)], pair_buf, s_pr.at[0], r_pr.at[0])
    swap.start()

    for copy in small_in:
        copy.wait()
    wk = wk_ref[...].astype(F32)
    queries = jnp.concatenate([rq_ref[...], cq_ref[...], jnp.zeros((6, width), F32)], 0)
    kvec = dot_nt(queries, wk, HIGH) * scale
    kr, kc = kvec[0:1], kvec[1:2]
    k_pieces = stack_rows(split(kr, 3) + split(kc, 3), width)
    ids = me_c * cols + lax.broadcasted_iota(jnp.int32, (1, cols), 1)

    swap.wait()
    chip_sum[...] = cot_loc[pl.ds(mine, half_n)] + pair_buf[...]
    rs_buf[me_chip] = chip_sum[me_chip]

    @pl.loop(1, half_n)
    def _(d):
        to_chips(lambda chip: chip_sum.at[chip], rs_buf.at[me_chip], s_rs, r_rs, d).start()

    @pl.loop(0, n_chunk)
    def _(k):
        local(cells_hbm, cells, cell_sem, k).wait()
        at = pl.ds(pl.multiple_of(k * chunk, chunk), chunk)
        s = dot_nt(k_pieces, cells[at].reshape(chunk * cols, width))
        one, two = [], []
        for i in range(chunk):
            x = s[:, i * cols : (i + 1) * cols]
            live = ids < counts[k * chunk + i]
            one.append(jnp.where(live, x[0:1] + x[1:2] + x[2:3], NEG_FILL))
            two.append(jnp.where(live, x[3:4] + x[4:5] + x[5:6], NEG_FILL))
        sr[at, :] = jnp.concatenate(one, 0)
        sc[at, :] = jnp.concatenate(two, 0)

    @pl.loop(1, half_n)
    def _(d):
        to_chips(lambda chip: chip_sum.at[chip], rs_buf.at[me_chip], s_rs, r_rs, d).wait_send()
        from_chips(lambda chip: rs_buf.at[chip], s_rs, r_rs, d).wait_recv()

    own = rs_buf[0]
    for i in range(1, half_n):
        own = own + rs_buf[i]
    cot_full[mine + me_chip] = own
    own_slot = cot_full.at[mine + me_chip]

    @pl.loop(1, half_n)
    def _(d):
        to_chips(lambda chip: own_slot, own_slot, s_ag, r_ag, d).start()


    score = sc[...]
    col_m = jnp.max(score, 0, keepdims=True)
    weight = jnp.where(score > 0.5 * NEG_FILL, jnp.exp(score - col_m), 0.0)
    wc[...] = weight
    col_t = jnp.sum(weight, 0, keepdims=True)
    for j, value in enumerate((col_m, col_t)):
        for i in range(q_rows):
            small[me_r, pl.ds(j * q_rows + i, 1), :] = value[:, i * 128 : (i + 1) * 128]
    small_x = (lambda peer: small.at[me_r], small, s_sm, r_sm)
    start_rows(*small_x)

    score = sr[...]
    row_m = jnp.max(score, 1, keepdims=True)
    row_weight = jnp.where(score > 0.5 * NEG_FILL, jnp.exp(score - row_m), 0.0)
    wr[...] = row_weight
    row_t = jnp.sum(row_weight, 1, keepdims=True)
    sub = lax.broadcasted_iota(jnp.int32, (chunk, 1), 0)

    @pl.loop(0, n_chunk)
    def _(k):
        at = pl.ds(pl.multiple_of(k * chunk, chunk), chunk)
        pieces = jnp.concatenate(split(wr[at, :], 2), 0).astype(BF16)
        acc = jnp.zeros((chunk, width), F32)
        for i in range(chunk):
            s = jnp.dot(pieces, cells[k * chunk + i], preferred_element_type=F32)
            acc = jnp.where(sub == i, s[0:chunk] + s[chunk : 2 * chunk], acc)
        row_pool[at, :] = acc

    row_buf[me_c, 0] = row_pool[...]
    row_buf[me_c, 1] = row_cot[...]
    row_buf[me_c, 2] = jnp.broadcast_to(row_m, (rows, width))
    row_buf[me_c, 3] = jnp.broadcast_to(row_t, (rows, width))
    row_x = (row_buf.at[me_c], row_buf, s_rx, r_rx)
    start_cols(*row_x)

    w_t = jnp.concatenate([p.T for p in split(weight, 2)], 1).astype(BF16)
    pick = lax.rem(lax.broadcasted_iota(jnp.int32, (2 * rows, 2 * width), 0), rows)
    lane = lax.broadcasted_iota(jnp.int32, (2 * rows, 2 * width), 1)
    pick = pick - jnp.where(lane < width, 0, 1)
    col_pool[...] = jnp.zeros_like(col_pool)

    @pl.loop(0, rows // 4)
    def _(k):
        acc = col_pool[...]
        for i in (0, 2):
            r = k * 4 + i
            one = jnp.where(pick == r, 1.0, 0.0).astype(BF16)
            spread = jnp.dot(w_t, one, preferred_element_type=F32)
            acc = acc + spread[:, :width] * cells[r].astype(F32)
            acc = acc + spread[:, width:] * cells[r + 1].astype(F32)
        col_pool[...] = acc

    wait_cols(*row_x)
    top = row_buf[0, 2]
    for i in range(1, n_col):
        top = jnp.maximum(top, row_buf[i, 2])
    pool = jnp.zeros((rows, width), F32)
    total = jnp.zeros((rows, width), F32)
    cot = jnp.zeros((rows, width), F32)
    for i in range(n_col):
        decay = jnp.exp(row_buf[i, 2] - top)
        pool = pool + row_buf[i, 0] * decay
        total = total + row_buf[i, 3] * decay
        cot = cot + row_buf[i, 1]
    factor = jnp.exp(row_buf[me_c, 2] - top) / total
    both = jnp.dot(wv_ref[...], wo_ref[...], preferred_element_type=F32)
    g_row = dot_nt(cot, both, HIGH)
    row_grad[...] = g_row
    row_dot = jnp.sum(pool * g_row, 1, keepdims=True) / total[:, 0:1]
    row_prob = wr[...] * factor[:, 0:1]

    @pl.loop(1, half_n)
    def _(d):
        to_chips(lambda chip: own_slot, own_slot, s_ag, r_ag, d).wait_send()
        from_chips(lambda chip: cot_full.at[mine + chip], s_ag, r_ag, d).wait_recv()

    half_at = cot_full.at[pl.ds(mine, half_n)]
    fill = to_sibling(half_at, half_at, s_pr.at[1], r_pr.at[1])
    fill.start()

    @pl.loop(0, n_chunk)
    def _(k):
        at = pl.ds(pl.multiple_of(k * chunk, chunk), chunk)
        pieces = jnp.concatenate(split(row_grad[at, :], 2), 0).astype(BF16)
        acc = jnp.zeros((chunk, cols), F32)
        for i in range(chunk):
            s = dot_nt(pieces, cells[k * chunk + i])
            acc = jnp.where(sub == i, s[0:chunk] + s[chunk : 2 * chunk], acc)
        rdp[at, :] = acc

    row_ds = row_prob * (rdp[...] - row_dot)
    sr[...] = row_ds

    wait_rows(*small_x)
    top = small[0, 0:q_rows]
    for i in range(1, n_row):
        top = jnp.maximum(top, small[i, 0:q_rows])
    total = jnp.zeros((q_rows, 128), F32)
    for i in range(n_row):
        total = total + small[i, q_rows : 2 * q_rows] * jnp.exp(small[i, 0:q_rows] - top)
    f_col = jnp.exp(col_m - flat_row(top)) / flat_row(total)
    col_prob = wc[...] * f_col
    wc[...] = col_prob
    f_t = jnp.broadcast_to(f_col, (8, cols)).T[:, 0:1]

    fill.wait_send()
    other_at = cot_full.at[pl.ds(other, half_n)]
    to_sibling(other_at, other_at, s_pr.at[1], r_pr.at[1]).wait_recv()
    cot_all = cot_full[...].reshape(cols, width)
    m_loc = dot_tn(col_pool[...] * f_t, cot_all, HIGH)
    m_loc = m_loc + dot_tn(row_pool[...] * factor, cot, HIGH)
    for i in range(n_row):
        red_src[i, 0:m_per] = m_loc[i * m_per : (i + 1) * m_per]
        if m_per < 8:
            red_src[i, m_per:8] = jnp.zeros((8 - m_per, width), F32)
    reduce = (lambda peer: red_src.at[peer], red_buf, s_rd, r_rd)
    start_rows(*reduce)
    red_buf[me_r] = red_src[me_r]

    g_col = dot_nt(cot_all, both, HIGH)
    g_out[...] = g_col

    @pl.loop(0, n_chunk)
    def _(k):
        at = pl.ds(pl.multiple_of(k * chunk, chunk), chunk)
        acc = jnp.zeros((16, cols), F32)
        for i in range(chunk):
            prod = cells[k * chunk + i].astype(F32) * g_out[...]
            hi = prod.astype(BF16)
            lo = (prod - hi.astype(F32)).astype(BF16)
            ones = jnp.where(sub16 == i, 1.0, 0.0).astype(BF16)
            acc = acc + dot_nt(ones, hi) + dot_nt(ones, lo)
        cdp[at, :] = acc[0:chunk]

    part_dot = jnp.sum(wc[...] * cdp[...], 0, keepdims=True)
    for i in range(q_rows):
        dots_buf[me_r, pl.ds(i, 1), :] = part_dot[:, i * 128 : (i + 1) * 128]
    dots_x = (lambda peer: dots_buf.at[me_r], dots_buf, s_dt, r_dt)
    start_rows(*dots_x)

    wait_rows(*reduce)
    acc = red_buf[0]
    for i in range(1, n_row):
        acc = acc + red_buf[i]
    part[me_c] = acc
    col_x = (part.at[me_c], part, s_cx, r_cx)
    start_cols(*col_x)

    wait_rows(*dots_x)
    dots = dots_buf[0, 0:q_rows]
    for i in range(1, n_row):
        dots = dots + dots_buf[i, 0:q_rows]
    col_ds = wc[...] * (cdp[...] - flat_row(dots))
    sc[...] = col_ds

    turn = lax.rem(lax.broadcasted_iota(jnp.int32, (4 * chunk, 1), 0), chunk)

    def moments(k, acc):
        at = pl.ds(pl.multiple_of(k * chunk, chunk), chunk)
        pieces = split(sr[at, :], 2) + split(sc[at, :], 2)
        pieces = jnp.concatenate(pieces, 0).astype(BF16)
        for i in range(chunk):
            s = jnp.dot(pieces, cells[k * chunk + i], preferred_element_type=F32)
            acc = acc + jnp.where(turn == i, s, 0.0)
        return acc

    acc = lax.fori_loop(0, n_chunk, moments, jnp.zeros((4 * chunk, width), F32))
    ab_buf[me_r] = jnp.concatenate(
        [
            jnp.sum(acc[0 : 2 * chunk], 0, keepdims=True),
            jnp.sum(acc[2 * chunk : 4 * chunk], 0, keepdims=True),
            jnp.zeros((6, width), F32),
        ],
        0,
    )
    ab_x = (lambda peer: ab_buf.at[me_r], ab_buf, s_ab, r_ab)
    start_rows(*ab_x)

    wait_cols(*col_x)
    acc = part[0]
    for i in range(1, n_col):
        acc = acc + part[i]
    m_full[me_r] = acc
    collect = (lambda peer: m_full.at[me_r], m_full, s_mg, r_mg)
    start_rows(*collect)

    pieces = [split(x, 2) for x in (row_prob, row_ds, col_ds, wc[...])]
    for half in range(2):
        block = jnp.concatenate([p[half] for p in pieces], 0)
        lhs_out[:, half * 4 * rows : (half + 1) * 4 * rows] = block.T.astype(BF16)
    zero = jnp.zeros((rows, width), F32)
    one = jnp.ones((rows, width), F32)
    left = jnp.concatenate(
        [g_row, jnp.broadcast_to(kr, (rows, width)), jnp.broadcast_to(kc, (rows, width)), zero], 0
    )
    right = jnp.concatenate([zero, zero, zero, one], 0)
    half = jnp.concatenate([left, right], 1)
    base_out[...] = jnp.concatenate([half, half], 0)

    wait_rows(*ab_x)
    acc = ab_buf[0]
    for i in range(1, n_row):
        acc = acc + ab_buf[i]
    ab_part[me_c] = acc
    ab_cx = (ab_part.at[me_c], ab_part, s_ac, r_ac)
    start_cols(*ab_cx)
    wait_rows(*collect)
    m_out[...] = jnp.concatenate([m_full[i, 0:m_per] for i in range(n_row)], 0)
    wait_cols(*ab_cx)
    acc = ab_part[0]
    for i in range(1, n_col):
        acc = acc + ab_part[i]
    ab_out[...] = acc


def cell_kernel(
    rows, lhs_ref, base_ref, g_ref, m_ref, ab_ref, wk_ref, wv_ref, wo_ref, rq_ref, cq_ref, up_ref,
    out_ref, kwg_ref, vwg_ref, owg_ref, rqg_ref, cqg_ref,
):
    block = up_ref.shape[0]
    width = up_ref.shape[2]
    step = pl.program_id(0)
    scale = 1.0 / math.sqrt(width)
    owner = lax.rem(lax.broadcasted_iota(jnp.int32, base_ref.shape, 0), rows)

    @pl.when(step == 0)
    def _():
        ab, m = ab_ref[...], m_ref[...]
        queries = jnp.concatenate([rq_ref[...], cq_ref[...], jnp.zeros((6, width), F32)], 0)
        kwg_ref[...] = dot_tn(ab, queries * scale, HIGH)
        q_grad = dot_nn(ab, wk_ref[...].astype(F32), HIGH) * scale
        rqg_ref[...] = q_grad[0:1]
        cqg_ref[...] = q_grad[1:2]
        vwg_ref[...] = dot_nt(m, wo_ref[...].astype(F32), HIGH)
        owg_ref[...] = dot_tn(wv_ref[...].astype(F32), m, HIGH)

    @pl.loop(0, block, unroll=4)
    def _(i):
        rhs = jnp.where(owner == step * block + i, base_ref[...], 0.0).astype(BF16)
        res = jnp.dot(lhs_ref[...], rhs, preferred_element_type=F32)
        delta = res[:, :width] + res[:, width:] * g_ref[...]
        out_ref[i] = (up_ref[i].astype(F32) + delta).astype(out_ref.dtype)


def on_device(n_row, n_col, cells, upstream, counts, wk, wv, wo, rq, cq):
    rows, cols, width = cells.shape
    chunk = 8
    per = cols // n_row
    rq, cq = rq.reshape(1, width), cq.reshape(1, width)
    vmem = pl.BlockSpec(memory_space=pltpu.VMEM)
    hbm = pl.BlockSpec(memory_space=pl.ANY)
    n_chunk = rows // chunk
    dma = pltpu.SemaphoreType.DMA
    f32 = lambda *shape: pltpu.VMEM(shape, F32)
    small_rows = -(-2 * (cols // 128) // 8) * 8
    dots_rows = -(-(cols // 128) // 8) * 8
    square = jax.ShapeDtypeStruct((width, width), F32)
    vector = jax.ShapeDtypeStruct((1, width), F32)
    half_n = n_row // 2
    over_row, over_col, over_chip = dma((n_row,)), dma((n_col,)), dma((half_n,))
    lhs, base, g_col, m, ab = pl.pallas_call(
        functools.partial(stats_kernel, n_row, n_col, chunk),
        out_shape=(
            jax.ShapeDtypeStruct((cols, 8 * rows), BF16),
            jax.ShapeDtypeStruct((8 * rows, 2 * width), F32),
            jax.ShapeDtypeStruct((cols, width), F32),
            square,
            jax.ShapeDtypeStruct((8, width), F32),
        ),
        in_specs=[hbm, hbm, pl.BlockSpec(memory_space=pltpu.SMEM)] + [hbm] * 5,
        out_specs=(vmem,) * 5,
        scratch_shapes=[
            pltpu.VMEM(cells.shape, BF16), pltpu.VMEM(cells.shape, BF16),
            f32(n_row, per, width), f32(half_n, per, width), f32(half_n, per, width),
            f32(half_n, per, width), f32(n_row, per, width),
            f32(rows, width),
            f32(rows, cols), f32(rows, cols), f32(rows, cols), f32(rows, cols),
            f32(rows, cols), f32(rows, cols),
            f32(rows, width), f32(rows, width), f32(cols, width),
            f32(n_col, 4, rows, width),
            f32(n_row, small_rows, 128), f32(n_row, dots_rows, 128),
            f32(n_row, 8, width), f32(n_row, 8, width), f32(n_col, 8, width),
            f32(n_row, 8, width),
            f32(n_row, 8, width), f32(n_col, 8, width),
            pltpu.VMEM(wk.shape, BF16), pltpu.VMEM(wv.shape, BF16), pltpu.VMEM(wo.shape, BF16),
            f32(1, width), f32(1, width),
            dma((n_chunk,)), dma((n_chunk,)), dma((5,)), dma((2,)), dma((2,)),
            over_chip, over_chip, over_chip, over_chip,
            over_col, over_col, over_row, over_row, over_row, over_row,
            over_row, over_row, over_col, over_col, over_row, over_row,
            over_row, over_row, over_col, over_col,
        ],
        compiler_params=pltpu.CompilerParams(
            collective_id=0, has_side_effects=True, vmem_limit_bytes=VMEM_BYTES
        ),
        name="hub_stats",
    )(cells, upstream, counts, wk, wv, wo, rq, cq)
    block = 8
    whole = lambda shape: pl.BlockSpec(shape, lambda i: (0,) * len(shape))
    cell_spec = pl.BlockSpec((block, cols, width), lambda i: (i, 0, 0))
    fixed = (lhs, base, g_col, m, ab, wk, wv, wo, rq, cq)
    cell_grad, kwg, vwg, owg, rqg, cqg = pl.pallas_call(
        functools.partial(cell_kernel, rows),
        grid=(rows // block,),
        out_shape=(
            jax.ShapeDtypeStruct(cells.shape, cells.dtype),
            square, square, square, vector, vector,
        ),
        in_specs=[whole(x.shape) for x in fixed] + [cell_spec],
        out_specs=(cell_spec,) + (whole((width, width)),) * 3 + (whole((1, width)),) * 2,
        compiler_params=pltpu.CompilerParams(vmem_limit_bytes=VMEM_BYTES),
        name="cell_grad",
    )(*fixed, upstream)
    return cell_grad, kwg, vwg, owg, rqg.reshape(width), cqg.reshape(width)


def solution(mesh):
    placed = (P("row", "col", None), P("row", "col", None), P("row"), P(), P(), P(), P(), P())
    return jax.shard_map(
        functools.partial(on_device, mesh.shape["row"], mesh.shape["col"]),
        mesh=mesh,
        in_specs=placed,
        out_specs=(P("row", "col", None), P(), P(), P(), P(), P()),
        check_vma=False,
    )
```

```python
import functools
import math

import jax
import jax.numpy as jnp
from jax import lax
from jax.experimental import pallas as pl
from jax.experimental.pallas import tpu as pltpu
from jax.sharding import PartitionSpec as P

NEG_FILL = -1e30
HIGH = lax.Precision.HIGHEST
MESH = pl.DeviceIdType.MESH
F32 = jnp.float32
BF16 = jnp.bfloat16
VMEM_BYTES = 62 * 1024 * 1024


def dot_nt(a, b, precision=None):
    return lax.dot_general(
        a, b, (((1,), (1,)), ((), ())), precision=precision, preferred_element_type=F32
    )


def dot_tn(a, b, precision=None):
    return lax.dot_general(
        a, b, (((0,), (0,)), ((), ())), precision=precision, preferred_element_type=F32
    )


def dot_nn(a, b, precision=None):
    return jnp.dot(a, b, precision=precision, preferred_element_type=F32)


def split(x, parts):
    pieces = []
    for _ in range(parts):
        piece = x.astype(BF16).astype(F32)
        pieces.append(piece)
        x = x - piece
    return pieces


def stack_rows(rows, width):
    pad = jnp.zeros((16 - len(rows), width), F32)
    return jnp.concatenate(rows + [pad], 0).astype(BF16)


def flat_row(tile):
    return jnp.concatenate([tile[i : i + 1] for i in range(tile.shape[0])], 1)


def stats_kernel(
    n_row, n_col, chunk,
    cells_hbm, up_hbm, counts, wk_hbm, wv_hbm, wo_hbm, rq_hbm, cq_hbm,
    raw_hbm, m_out, ab_out,
    lhs_out, base_out, g_out,
    cells, up, cot_loc, pair_buf, chip_sum, rs_buf, cot_full, row_cot, sr, sc, wr, wc, rdp, cdp,
    row_pool, row_grad, col_pool, row_buf, small, dots_buf, red_src, red_buf, part, m_full,
    ab_buf, ab_part, wk_ref, wv_ref, wo_ref, rq_ref, cq_ref,
    cell_sem, up_sem, in_sem, out_sem, s_pr, r_pr, s_rs, r_rs, s_ag, r_ag, s_rx, r_rx, s_sm, r_sm, s_dt, r_dt,
    s_rd, r_rd, s_cx, r_cx, s_mg, r_mg, s_ab, r_ab, s_ac, r_ac,
):
    rows, cols, width = cells.shape
    scale = 1.0 / math.sqrt(width)
    me_r = lax.axis_index("row")
    me_c = lax.axis_index("col")
    n_chunk = rows // chunk
    per = cols // n_row
    m_per = width // n_row
    q_rows = cols // 128

    def local(hbm, vmem, sem, k):
        return pltpu.make_async_copy(
            hbm.at[pl.ds(k * chunk, chunk)], vmem.at[pl.ds(k * chunk, chunk)], sem.at[k]
        )

    for k in range(n_chunk):
        local(up_hbm, up, up_sem, k).start()
    small_in = [
        pltpu.make_async_copy(src, dst, in_sem.at[i])
        for i, (src, dst) in enumerate(
            ((wk_hbm, wk_ref), (wv_hbm, wv_ref), (wo_hbm, wo_ref), (rq_hbm, rq_ref), (cq_hbm, cq_ref))
        )
    ]
    for copy in small_in:
        copy.start()
    for k in range(n_chunk):
        local(cells_hbm, cells, cell_sem, k).start()
    sub16 = lax.broadcasted_iota(jnp.int32, (16, 2 * width), 0)

    barrier = pltpu.get_barrier_semaphore()

    @pl.loop(1, n_row)
    def _(d):
        pl.semaphore_signal(
            barrier, inc=1, device_id=(lax.rem(me_r + d, n_row), me_c), device_id_type=MESH
        )

    @pl.loop(1, n_col)
    def _(d):
        pl.semaphore_signal(
            barrier, inc=1, device_id=(me_r, lax.rem(me_c + d, n_col)), device_id_type=MESH
        )

    def to_rows(src_of, dst, s_sem, r_sem, d):
        peer = lax.rem(me_r + d, n_row)
        return pltpu.make_async_remote_copy(
            src_ref=src_of(peer), dst_ref=dst.at[me_r], send_sem=s_sem.at[d],
            recv_sem=r_sem.at[d], device_id=(peer, me_c), device_id_type=MESH,
        )

    def from_rows(src_of, dst, s_sem, r_sem, d):
        peer = lax.rem(me_r + n_row - d, n_row)
        return pltpu.make_async_remote_copy(
            src_ref=src_of(peer), dst_ref=dst.at[peer], send_sem=s_sem.at[d],
            recv_sem=r_sem.at[d], device_id=(peer, me_c), device_id_type=MESH,
        )

    def to_cols(src, dst, s_sem, r_sem, d):
        peer = lax.rem(me_c + d, n_col)
        return pltpu.make_async_remote_copy(
            src_ref=src, dst_ref=dst.at[me_c], send_sem=s_sem.at[d],
            recv_sem=r_sem.at[d], device_id=(me_r, peer), device_id_type=MESH,
        )

    def from_cols(src, dst, s_sem, r_sem, d):
        peer = lax.rem(me_c + n_col - d, n_col)
        return pltpu.make_async_remote_copy(
            src_ref=src, dst_ref=dst.at[peer], send_sem=s_sem.at[d],
            recv_sem=r_sem.at[d], device_id=(me_r, peer), device_id_type=MESH,
        )

    half_n = n_row // 2
    me_core, me_chip = lax.rem(me_r, 2), lax.div(me_r, 2)
    mine, other = me_core * half_n, (1 - me_core) * half_n

    def to_sibling(src, dst, s_sem, r_sem):
        return pltpu.make_async_remote_copy(
            src_ref=src, dst_ref=dst, send_sem=s_sem, recv_sem=r_sem,
            device_id=(me_r + 1 - 2 * me_core, me_c), device_id_type=MESH,
        )

    def to_chips(src_of, dst, s_sem, r_sem, d):
        chip = lax.rem(me_chip + d, half_n)
        return pltpu.make_async_remote_copy(
            src_ref=src_of(chip), dst_ref=dst, send_sem=s_sem.at[d], recv_sem=r_sem.at[d],
            device_id=(chip * 2 + me_core, me_c), device_id_type=MESH,
        )

    def from_chips(dst_of, s_sem, r_sem, d):
        chip = lax.rem(me_chip + half_n - d, half_n)
        return pltpu.make_async_remote_copy(
            src_ref=dst_of(chip), dst_ref=dst_of(chip), send_sem=s_sem.at[d],
            recv_sem=r_sem.at[d], device_id=(chip * 2 + me_core, me_c), device_id_type=MESH,
        )

    def start_rows(*args):
        @pl.loop(1, n_row)
        def _(d):
            to_rows(*args, d).start()

    def wait_rows(*args):
        @pl.loop(1, n_row)
        def _(d):
            to_rows(*args, d).wait_send()
            from_rows(*args, d).wait_recv()

    def start_cols(*args):
        @pl.loop(1, n_col)
        def _(d):
            to_cols(*args, d).start()

    def wait_cols(*args):
        @pl.loop(1, n_col)
        def _(d):
            to_cols(*args, d).wait_send()
            from_cols(*args, d).wait_recv()

    span = 64
    groups = span // per
    for k in range(n_chunk):
        local(up_hbm, up, up_sem, k).wait()

        def add_block(cb, total, k=k):
            x = up[pl.ds(k * chunk, chunk), pl.ds(pl.multiple_of(cb * span, span), span), :]
            x = x.astype(F32)
            by_col = jnp.sum(x, 0).reshape(groups, per, width)
            at = pl.ds(cb * groups, groups)
            cot_loc[at] = by_col if k == 0 else cot_loc[at] + by_col
            return total + jnp.sum(x, 1)

        row_cot[pl.ds(k * chunk, chunk), :] = lax.fori_loop(
            0, cols // span, add_block, jnp.zeros((chunk, width), F32)
        )

    pl.semaphore_wait(barrier, n_row + n_col - 2)
    swap = to_sibling(cot_loc.at[pl.ds(other, half_n)], pair_buf, s_pr.at[0], r_pr.at[0])
    swap.start()

    for copy in small_in:
        copy.wait()
    wk = wk_ref[...].astype(F32)
    queries = jnp.concatenate([rq_ref[...], cq_ref[...], jnp.zeros((6, width), F32)], 0)
    kvec = dot_nt(queries, wk, HIGH) * scale
    kr, kc = kvec[0:1], kvec[1:2]
    k_pieces = stack_rows(split(kr, 3) + split(kc, 3), width)
    ids = me_c * cols + lax.broadcasted_iota(jnp.int32, (1, cols), 1)

    swap.wait()
    chip_sum[...] = cot_loc[pl.ds(mine, half_n)] + pair_buf[...]
    rs_buf[me_chip] = chip_sum[me_chip]

    @pl.loop(1, half_n)
    def _(d):
        to_chips(lambda chip: chip_sum.at[chip], rs_buf.at[me_chip], s_rs, r_rs, d).start()

    @pl.loop(0, n_chunk)
    def _(k):
        local(cells_hbm, cells, cell_sem, k).wait()
        at = pl.ds(pl.multiple_of(k * chunk, chunk), chunk)
        s = dot_nt(k_pieces, cells[at].reshape(chunk * cols, width))
        one, two = [], []
        for i in range(chunk):
            x = s[:, i * cols : (i + 1) * cols]
            live = ids < counts[k * chunk + i]
            one.append(jnp.where(live, x[0:1] + x[1:2] + x[2:3], NEG_FILL))
            two.append(jnp.where(live, x[3:4] + x[4:5] + x[5:6], NEG_FILL))
        sr[at, :] = jnp.concatenate(one, 0)
        sc[at, :] = jnp.concatenate(two, 0)

    @pl.loop(1, half_n)
    def _(d):
        to_chips(lambda chip: chip_sum.at[chip], rs_buf.at[me_chip], s_rs, r_rs, d).wait_send()
        from_chips(lambda chip: rs_buf.at[chip], s_rs, r_rs, d).wait_recv()

    own = rs_buf[0]
    for i in range(1, half_n):
        own = own + rs_buf[i]
    cot_full[mine + me_chip] = own
    own_slot = cot_full.at[mine + me_chip]

    @pl.loop(1, half_n)
    def _(d):
        to_chips(lambda chip: own_slot, own_slot, s_ag, r_ag, d).start()


    score = sc[...]
    col_m = jnp.max(score, 0, keepdims=True)
    weight = jnp.where(score > 0.5 * NEG_FILL, jnp.exp(score - col_m), 0.0)
    wc[...] = weight
    col_t = jnp.sum(weight, 0, keepdims=True)
    for j, value in enumerate((col_m, col_t)):
        for i in range(q_rows):
            small[me_r, pl.ds(j * q_rows + i, 1), :] = value[:, i * 128 : (i + 1) * 128]
    small_x = (lambda peer: small.at[me_r], small, s_sm, r_sm)
    start_rows(*small_x)

    score = sr[...]
    row_m = jnp.max(score, 1, keepdims=True)
    row_weight = jnp.where(score > 0.5 * NEG_FILL, jnp.exp(score - row_m), 0.0)
    wr[...] = row_weight
    row_t = jnp.sum(row_weight, 1, keepdims=True)
    sub = lax.broadcasted_iota(jnp.int32, (chunk, 1), 0)

    @pl.loop(0, n_chunk)
    def _(k):
        at = pl.ds(pl.multiple_of(k * chunk, chunk), chunk)
        pieces = jnp.concatenate(split(wr[at, :], 2), 0).astype(BF16)
        acc = jnp.zeros((chunk, width), F32)
        for i in range(chunk):
            s = jnp.dot(pieces, cells[k * chunk + i], preferred_element_type=F32)
            acc = jnp.where(sub == i, s[0:chunk] + s[chunk : 2 * chunk], acc)
        row_pool[at, :] = acc

    row_buf[me_c, 0] = row_pool[...]
    row_buf[me_c, 1] = row_cot[...]
    row_buf[me_c, 2] = jnp.broadcast_to(row_m, (rows, width))
    row_buf[me_c, 3] = jnp.broadcast_to(row_t, (rows, width))
    row_x = (row_buf.at[me_c], row_buf, s_rx, r_rx)
    start_cols(*row_x)

    w_t = jnp.concatenate([p.T for p in split(weight, 2)], 1).astype(BF16)
    pick = lax.rem(lax.broadcasted_iota(jnp.int32, (2 * rows, 2 * width), 0), rows)
    lane = lax.broadcasted_iota(jnp.int32, (2 * rows, 2 * width), 1)
    pick = pick - jnp.where(lane < width, 0, 1)
    col_pool[...] = jnp.zeros_like(col_pool)

    @pl.loop(0, rows // 4)
    def _(k):
        acc = col_pool[...]
        for i in (0, 2):
            r = k * 4 + i
            one = jnp.where(pick == r, 1.0, 0.0).astype(BF16)
            spread = jnp.dot(w_t, one, preferred_element_type=F32)
            acc = acc + spread[:, :width] * cells[r].astype(F32)
            acc = acc + spread[:, width:] * cells[r + 1].astype(F32)
        col_pool[...] = acc

    wait_cols(*row_x)
    top = row_buf[0, 2]
    for i in range(1, n_col):
        top = jnp.maximum(top, row_buf[i, 2])
    pool = jnp.zeros((rows, width), F32)
    total = jnp.zeros((rows, width), F32)
    cot = jnp.zeros((rows, width), F32)
    for i in range(n_col):
        decay = jnp.exp(row_buf[i, 2] - top)
        pool = pool + row_buf[i, 0] * decay
        total = total + row_buf[i, 3] * decay
        cot = cot + row_buf[i, 1]
    factor = jnp.exp(row_buf[me_c, 2] - top) / total
    both = jnp.dot(wv_ref[...], wo_ref[...], preferred_element_type=F32)
    g_row = dot_nt(cot, both, HIGH)
    row_grad[...] = g_row
    row_dot = jnp.sum(pool * g_row, 1, keepdims=True) / total[:, 0:1]
    row_prob = wr[...] * factor[:, 0:1]

    @pl.loop(1, half_n)
    def _(d):
        to_chips(lambda chip: own_slot, own_slot, s_ag, r_ag, d).wait_send()
        from_chips(lambda chip: cot_full.at[mine + chip], s_ag, r_ag, d).wait_recv()

    half_at = cot_full.at[pl.ds(mine, half_n)]
    fill = to_sibling(half_at, half_at, s_pr.at[1], r_pr.at[1])
    fill.start()

    @pl.loop(0, n_chunk)
    def _(k):
        at = pl.ds(pl.multiple_of(k * chunk, chunk), chunk)
        pieces = jnp.concatenate(split(row_grad[at, :], 2), 0).astype(BF16)
        acc = jnp.zeros((chunk, cols), F32)
        for i in range(chunk):
            s = dot_nt(pieces, cells[k * chunk + i])
            acc = jnp.where(sub == i, s[0:chunk] + s[chunk : 2 * chunk], acc)
        rdp[at, :] = acc

    row_ds = row_prob * (rdp[...] - row_dot)
    sr[...] = row_ds

    wait_rows(*small_x)
    top = small[0, 0:q_rows]
    for i in range(1, n_row):
        top = jnp.maximum(top, small[i, 0:q_rows])
    total = jnp.zeros((q_rows, 128), F32)
    for i in range(n_row):
        total = total + small[i, q_rows : 2 * q_rows] * jnp.exp(small[i, 0:q_rows] - top)
    f_col = jnp.exp(col_m - flat_row(top)) / flat_row(total)
    col_prob = wc[...] * f_col
    wc[...] = col_prob
    f_t = jnp.broadcast_to(f_col, (8, cols)).T[:, 0:1]

    fill.wait_send()
    other_at = cot_full.at[pl.ds(other, half_n)]
    to_sibling(other_at, other_at, s_pr.at[1], r_pr.at[1]).wait_recv()
    cot_all = cot_full[...].reshape(cols, width)
    m_loc = dot_tn(col_pool[...] * f_t, cot_all, HIGH)
    m_loc = m_loc + dot_tn(row_pool[...] * factor, cot, HIGH)
    for i in range(n_row):
        red_src[i, 0:m_per] = m_loc[i * m_per : (i + 1) * m_per]
        if m_per < 8:
            red_src[i, m_per:8] = jnp.zeros((8 - m_per, width), F32)
    reduce = (lambda peer: red_src.at[peer], red_buf, s_rd, r_rd)
    start_rows(*reduce)
    red_buf[me_r] = red_src[me_r]

    g_col = dot_nt(cot_all, both, HIGH)
    g_out[...] = g_col

    @pl.loop(0, n_chunk)
    def _(k):
        at = pl.ds(pl.multiple_of(k * chunk, chunk), chunk)
        acc = jnp.zeros((16, cols), F32)
        for i in range(chunk):
            prod = cells[k * chunk + i].astype(F32) * g_out[...]
            hi = prod.astype(BF16)
            lo = (prod - hi.astype(F32)).astype(BF16)
            ones = jnp.where(sub16 == i, 1.0, 0.0).astype(BF16)
            acc = acc + dot_nt(ones, jnp.concatenate([hi, lo], 1))
        cdp[at, :] = acc[0:chunk]

    part_dot = jnp.sum(wc[...] * cdp[...], 0, keepdims=True)
    for i in range(q_rows):
        dots_buf[me_r, pl.ds(i, 1), :] = part_dot[:, i * 128 : (i + 1) * 128]
    dots_x = (lambda peer: dots_buf.at[me_r], dots_buf, s_dt, r_dt)
    start_rows(*dots_x)

    wait_rows(*reduce)
    acc = red_buf[0]
    for i in range(1, n_row):
        acc = acc + red_buf[i]
    part[me_c] = acc
    col_x = (part.at[me_c], part, s_cx, r_cx)
    start_cols(*col_x)

    wait_rows(*dots_x)
    dots = dots_buf[0, 0:q_rows]
    for i in range(1, n_row):
        dots = dots + dots_buf[i, 0:q_rows]
    col_ds = wc[...] * (cdp[...] - flat_row(dots))
    sc[...] = col_ds

    turn = lax.rem(lax.broadcasted_iota(jnp.int32, (4 * chunk, 1), 0), chunk)

    def moments(k, acc):
        at = pl.ds(pl.multiple_of(k * chunk, chunk), chunk)
        pieces = split(sr[at, :], 2) + split(sc[at, :], 2)
        pieces = jnp.concatenate(pieces, 0).astype(BF16)
        for i in range(chunk):
            s = jnp.dot(pieces, cells[k * chunk + i], preferred_element_type=F32)
            acc = acc + jnp.where(turn == i, s, 0.0)
        return acc

    acc = lax.fori_loop(0, n_chunk, moments, jnp.zeros((4 * chunk, width), F32))
    ab_buf[me_r] = jnp.concatenate(
        [
            jnp.sum(acc[0 : 2 * chunk], 0, keepdims=True),
            jnp.sum(acc[2 * chunk : 4 * chunk], 0, keepdims=True),
            jnp.zeros((6, width), F32),
        ],
        0,
    )
    ab_x = (lambda peer: ab_buf.at[me_r], ab_buf, s_ab, r_ab)
    start_rows(*ab_x)

    wait_cols(*col_x)
    acc = part[0]
    for i in range(1, n_col):
        acc = acc + part[i]
    m_full[me_r] = acc
    collect = (lambda peer: m_full.at[me_r], m_full, s_mg, r_mg)
    start_rows(*collect)

    pieces = [split(x, 2) for x in (row_prob, row_ds, col_ds, wc[...])]
    for half in range(2):
        block = jnp.concatenate([p[half] for p in pieces], 0)
        lhs_out[:, half * 4 * rows : (half + 1) * 4 * rows] = block.T.astype(BF16)
    zero = jnp.zeros((rows, width), F32)
    one = jnp.ones((rows, width), F32)
    left = jnp.concatenate(
        [g_row, jnp.broadcast_to(kr, (rows, width)), jnp.broadcast_to(kc, (rows, width)), zero], 0
    )
    right = jnp.concatenate([zero, zero, zero, one], 0)
    half = jnp.concatenate([left, right], 1)
    base_out[...] = jnp.concatenate([half, half], 0)

    owner = lax.rem(lax.broadcasted_iota(jnp.int32, base_out.shape, 0), rows)

    def write(k):
        at = pl.ds(k * chunk, chunk)
        return pltpu.make_async_copy(up.at[at], raw_hbm.at[at], out_sem.at[k])

    def cell_grads(first, last):
        @pl.loop(first, last)
        def _(k):
            for i in range(chunk):
                r = k * chunk + i
                rhs = jnp.where(owner == r, base_out[...], 0.0).astype(BF16)
                res = jnp.dot(lhs_out[...], rhs, preferred_element_type=F32)
                delta = res[:, :width] + res[:, width:] * g_out[...]
                up[r] = (up[r].astype(F32) + delta).astype(BF16)
            write(k).start()

    cell_grads(0, n_chunk // 2)

    wait_rows(*ab_x)
    acc = ab_buf[0]
    for i in range(1, n_row):
        acc = acc + ab_buf[i]
    ab_part[me_c] = acc
    ab_cx = (ab_part.at[me_c], ab_part, s_ac, r_ac)
    start_cols(*ab_cx)
    cell_grads(n_chunk // 2, n_chunk)
    wait_rows(*collect)
    m_out[...] = jnp.concatenate([m_full[i, 0:m_per] for i in range(n_row)], 0)
    wait_cols(*ab_cx)
    acc = ab_part[0]
    for i in range(1, n_col):
        acc = acc + ab_part[i]
    ab_out[...] = acc
    for k in range(n_chunk):
        write(k).wait()


def finish_kernel(
    pieces, raw_hbm, m_ref, ab_ref, wk_ref, wv_ref, wo_ref, rq_ref, cq_ref,
    out_hbm, kwg_ref, vwg_ref, owg_ref, rqg_ref, cqg_ref, sems,
):
    size = raw_hbm.shape[0] // pieces
    width = m_ref.shape[0]
    scale = 1.0 / math.sqrt(width)
    moves = [
        pltpu.make_async_copy(
            raw_hbm.at[pl.ds(i * size, size)], out_hbm.at[pl.ds(i * size, size)], sems.at[i]
        )
        for i in range(pieces)
    ]
    for move in moves:
        move.start()
    ab, m = ab_ref[...], m_ref[...]
    queries = jnp.concatenate([rq_ref[...], cq_ref[...], jnp.zeros((6, width), F32)], 0)
    kwg_ref[...] = dot_tn(ab, queries * scale, HIGH)
    q_grad = dot_nn(ab, wk_ref[...].astype(F32), HIGH) * scale
    rqg_ref[...] = q_grad[0:1]
    cqg_ref[...] = q_grad[1:2]
    vwg_ref[...] = dot_nt(m, wo_ref[...].astype(F32), HIGH)
    owg_ref[...] = dot_tn(wv_ref[...].astype(F32), m, HIGH)
    for move in moves:
        move.wait()


def on_device(n_row, n_col, cells, upstream, counts, wk, wv, wo, rq, cq):
    rows, cols, width = cells.shape
    chunk = 8
    per = cols // n_row
    rq, cq = rq.reshape(1, width), cq.reshape(1, width)
    vmem = pl.BlockSpec(memory_space=pltpu.VMEM)
    hbm = pl.BlockSpec(memory_space=pl.ANY)
    n_chunk = rows // chunk
    dma = pltpu.SemaphoreType.DMA
    f32 = lambda *shape: pltpu.VMEM(shape, F32)
    small_rows = -(-2 * (cols // 128) // 8) * 8
    dots_rows = -(-(cols // 128) // 8) * 8
    square = jax.ShapeDtypeStruct((width, width), F32)
    vector = jax.ShapeDtypeStruct((1, width), F32)
    half_n = n_row // 2
    over_row, over_col, over_chip = dma((n_row,)), dma((n_col,)), dma((half_n,))
    raw, m, ab = pl.pallas_call(
        functools.partial(stats_kernel, n_row, n_col, chunk),
        out_shape=(
            jax.ShapeDtypeStruct(cells.shape, BF16),
            square,
            jax.ShapeDtypeStruct((8, width), F32),
        ),
        in_specs=[hbm, hbm, pl.BlockSpec(memory_space=pltpu.SMEM)] + [hbm] * 5,
        out_specs=(hbm, vmem, vmem),
        scratch_shapes=[
            pltpu.VMEM((cols, 8 * rows), BF16), f32(8 * rows, 2 * width), f32(cols, width),
            pltpu.VMEM(cells.shape, BF16), pltpu.VMEM(cells.shape, BF16),
            f32(n_row, per, width), f32(half_n, per, width), f32(half_n, per, width),
            f32(half_n, per, width), f32(n_row, per, width),
            f32(rows, width),
            f32(rows, cols), f32(rows, cols), f32(rows, cols), f32(rows, cols),
            f32(rows, cols), f32(rows, cols),
            f32(rows, width), f32(rows, width), f32(cols, width),
            f32(n_col, 4, rows, width),
            f32(n_row, small_rows, 128), f32(n_row, dots_rows, 128),
            f32(n_row, 8, width), f32(n_row, 8, width), f32(n_col, 8, width),
            f32(n_row, 8, width),
            f32(n_row, 8, width), f32(n_col, 8, width),
            pltpu.VMEM(wk.shape, BF16), pltpu.VMEM(wv.shape, BF16), pltpu.VMEM(wo.shape, BF16),
            f32(1, width), f32(1, width),
            dma((n_chunk,)), dma((n_chunk,)), dma((5,)), dma((n_chunk,)),
            dma((2,)), dma((2,)),
            over_chip, over_chip, over_chip, over_chip,
            over_col, over_col, over_row, over_row, over_row, over_row,
            over_row, over_row, over_col, over_col, over_row, over_row,
            over_row, over_row, over_col, over_col,
        ],
        compiler_params=pltpu.CompilerParams(
            collective_id=0, has_side_effects=True, vmem_limit_bytes=VMEM_BYTES
        ),
        name="hub_stats",
    )(cells, upstream, counts, wk, wv, wo, rq, cq)
    pieces = 16
    cell_grad, kwg, vwg, owg, rqg, cqg = pl.pallas_call(
        functools.partial(finish_kernel, pieces),
        out_shape=(
            jax.ShapeDtypeStruct(cells.shape, cells.dtype),
            square, square, square, vector, vector,
        ),
        in_specs=[hbm] + [vmem] * 7,
        out_specs=(hbm,) + (vmem,) * 5,
        scratch_shapes=[dma((pieces,))],
        compiler_params=pltpu.CompilerParams(vmem_limit_bytes=VMEM_BYTES),
        name="finish",
    )(raw, m, ab, wk, wv, wo, rq, cq)
    return cell_grad, kwg, vwg, owg, rqg.reshape(width), cqg.reshape(width)


def solution(mesh):
    placed = (P("row", "col", None), P("row", "col", None), P("row"), P(), P(), P(), P(), P())
    return jax.shard_map(
        functools.partial(on_device, mesh.shape["row"], mesh.shape["col"]),
        mesh=mesh,
        in_specs=placed,
        out_specs=(P("row", "col", None), P(), P(), P(), P(), P()),
        check_vma=False,
    )
```

```python
import functools
import math

import jax
import jax.numpy as jnp
from jax import lax
from jax.experimental import pallas as pl
from jax.experimental.pallas import tpu as pltpu
from jax.sharding import PartitionSpec as P

NEG_FILL = -1e30
HIGH = lax.Precision.HIGHEST
MESH = pl.DeviceIdType.MESH
F32 = jnp.float32
BF16 = jnp.bfloat16
VMEM_BYTES = 62 * 1024 * 1024


def dot_nt(a, b, precision=None):
    return lax.dot_general(
        a, b, (((1,), (1,)), ((), ())), precision=precision, preferred_element_type=F32
    )


def dot_tn(a, b, precision=None):
    return lax.dot_general(
        a, b, (((0,), (0,)), ((), ())), precision=precision, preferred_element_type=F32
    )


def dot_nn(a, b, precision=None):
    return jnp.dot(a, b, precision=precision, preferred_element_type=F32)


def split(x, parts):
    pieces = []
    for _ in range(parts):
        piece = x.astype(BF16).astype(F32)
        pieces.append(piece)
        x = x - piece
    return pieces


def stack_rows(rows, width):
    pad = jnp.zeros((16 - len(rows), width), F32)
    return jnp.concatenate(rows + [pad], 0).astype(BF16)


def flat_row(tile):
    return jnp.concatenate([tile[i : i + 1] for i in range(tile.shape[0])], 1)


def stats_kernel(
    n_row, n_col, chunk,
    cells_hbm, up_hbm, counts, wk_hbm, wv_hbm, wo_hbm, rq_hbm, cq_hbm,
    raw_hbm, m_out, ab_out,
    lhs_out, base_out, g_out,
    cells, up, cot_loc, pair_buf, chip_sum, rs_buf, cot_full, row_cot, sr, sc, wr, wc, rdp, cdp,
    row_pool, row_grad, col_pool, row_buf, small, dots_buf, red_src, red_buf, part, m_full,
    ab_buf, ab_part, wk_ref, wv_ref, wo_ref, rq_ref, cq_ref,
    cell_sem, up_sem, in_sem, out_sem, s_pr, r_pr, s_rs, r_rs, s_ag, r_ag, s_rx, r_rx, s_sm, r_sm, s_dt, r_dt,
    s_rd, r_rd, s_cx, r_cx, s_mg, r_mg, s_ab, r_ab, s_ac, r_ac,
):
    rows, cols, width = cells.shape
    scale = 1.0 / math.sqrt(width)
    me_r = lax.axis_index("row")
    me_c = lax.axis_index("col")
    n_chunk = rows // chunk
    per = cols // n_row
    m_per = width // n_row
    q_rows = cols // 128

    def local(hbm, vmem, sem, k):
        return pltpu.make_async_copy(
            hbm.at[pl.ds(k * chunk, chunk)], vmem.at[pl.ds(k * chunk, chunk)], sem.at[k]
        )

    for k in range(n_chunk):
        local(up_hbm, up, up_sem, k).start()
    small_in = [
        pltpu.make_async_copy(src, dst, in_sem.at[i])
        for i, (src, dst) in enumerate(
            ((wk_hbm, wk_ref), (wv_hbm, wv_ref), (wo_hbm, wo_ref), (rq_hbm, rq_ref), (cq_hbm, cq_ref))
        )
    ]
    for copy in small_in:
        copy.start()
    for k in range(n_chunk):
        local(cells_hbm, cells, cell_sem, k).start()
    sub16 = lax.broadcasted_iota(jnp.int32, (16, 2 * width), 0)

    barrier = pltpu.get_barrier_semaphore()

    @pl.loop(1, n_row)
    def _(d):
        pl.semaphore_signal(
            barrier, inc=1, device_id=(lax.rem(me_r + d, n_row), me_c), device_id_type=MESH
        )

    @pl.loop(1, n_col)
    def _(d):
        pl.semaphore_signal(
            barrier, inc=1, device_id=(me_r, lax.rem(me_c + d, n_col)), device_id_type=MESH
        )

    def to_rows(src_of, dst, s_sem, r_sem, d):
        peer = lax.rem(me_r + d, n_row)
        return pltpu.make_async_remote_copy(
            src_ref=src_of(peer), dst_ref=dst.at[me_r], send_sem=s_sem.at[d],
            recv_sem=r_sem.at[d], device_id=(peer, me_c), device_id_type=MESH,
        )

    def from_rows(src_of, dst, s_sem, r_sem, d):
        peer = lax.rem(me_r + n_row - d, n_row)
        return pltpu.make_async_remote_copy(
            src_ref=src_of(peer), dst_ref=dst.at[peer], send_sem=s_sem.at[d],
            recv_sem=r_sem.at[d], device_id=(peer, me_c), device_id_type=MESH,
        )

    def to_cols(src, dst, s_sem, r_sem, d):
        peer = lax.rem(me_c + d, n_col)
        return pltpu.make_async_remote_copy(
            src_ref=src, dst_ref=dst.at[me_c], send_sem=s_sem.at[d],
            recv_sem=r_sem.at[d], device_id=(me_r, peer), device_id_type=MESH,
        )

    def from_cols(src, dst, s_sem, r_sem, d):
        peer = lax.rem(me_c + n_col - d, n_col)
        return pltpu.make_async_remote_copy(
            src_ref=src, dst_ref=dst.at[peer], send_sem=s_sem.at[d],
            recv_sem=r_sem.at[d], device_id=(me_r, peer), device_id_type=MESH,
        )

    half_n = n_row // 2
    me_core, me_chip = lax.rem(me_r, 2), lax.div(me_r, 2)
    mine, other = me_core * half_n, (1 - me_core) * half_n

    def to_sibling(src, dst, s_sem, r_sem):
        return pltpu.make_async_remote_copy(
            src_ref=src, dst_ref=dst, send_sem=s_sem, recv_sem=r_sem,
            device_id=(me_r + 1 - 2 * me_core, me_c), device_id_type=MESH,
        )

    def to_chips(src_of, dst, s_sem, r_sem, d):
        chip = lax.rem(me_chip + d, half_n)
        return pltpu.make_async_remote_copy(
            src_ref=src_of(chip), dst_ref=dst, send_sem=s_sem.at[d], recv_sem=r_sem.at[d],
            device_id=(chip * 2 + me_core, me_c), device_id_type=MESH,
        )

    def from_chips(dst_of, s_sem, r_sem, d):
        chip = lax.rem(me_chip + half_n - d, half_n)
        return pltpu.make_async_remote_copy(
            src_ref=dst_of(chip), dst_ref=dst_of(chip), send_sem=s_sem.at[d],
            recv_sem=r_sem.at[d], device_id=(chip * 2 + me_core, me_c), device_id_type=MESH,
        )

    def start_rows(*args):
        @pl.loop(1, n_row)
        def _(d):
            to_rows(*args, d).start()

    def wait_rows(*args):
        @pl.loop(1, n_row)
        def _(d):
            to_rows(*args, d).wait_send()
            from_rows(*args, d).wait_recv()

    def start_cols(*args):
        @pl.loop(1, n_col)
        def _(d):
            to_cols(*args, d).start()

    def wait_cols(*args):
        @pl.loop(1, n_col)
        def _(d):
            to_cols(*args, d).wait_send()
            from_cols(*args, d).wait_recv()

    span = 64
    groups = span // per
    for k in range(n_chunk):
        local(up_hbm, up, up_sem, k).wait()

        def add_block(cb, total, k=k):
            x = up[pl.ds(k * chunk, chunk), pl.ds(pl.multiple_of(cb * span, span), span), :]
            x = x.astype(F32)
            by_col = jnp.sum(x, 0).reshape(groups, per, width)
            at = pl.ds(cb * groups, groups)
            cot_loc[at] = by_col if k == 0 else cot_loc[at] + by_col
            return total + jnp.sum(x, 1)

        row_cot[pl.ds(k * chunk, chunk), :] = lax.fori_loop(
            0, cols // span, add_block, jnp.zeros((chunk, width), F32)
        )

    pl.semaphore_wait(barrier, n_row + n_col - 2)
    swap = to_sibling(cot_loc.at[pl.ds(other, half_n)], pair_buf, s_pr.at[0], r_pr.at[0])
    swap.start()

    for copy in small_in:
        copy.wait()
    wk = wk_ref[...].astype(F32)
    queries = jnp.concatenate([rq_ref[...], cq_ref[...], jnp.zeros((6, width), F32)], 0)
    kvec = dot_nt(queries, wk, HIGH) * scale
    kr, kc = kvec[0:1], kvec[1:2]
    k_pieces = stack_rows(split(kr, 3) + split(kc, 3), width)
    ids = me_c * cols + lax.broadcasted_iota(jnp.int32, (1, cols), 1)

    swap.wait()
    chip_sum[...] = cot_loc[pl.ds(mine, half_n)] + pair_buf[...]
    rs_buf[me_chip] = chip_sum[me_chip]

    @pl.loop(1, half_n)
    def _(d):
        to_chips(lambda chip: chip_sum.at[chip], rs_buf.at[me_chip], s_rs, r_rs, d).start()

    @pl.loop(0, n_chunk)
    def _(k):
        local(cells_hbm, cells, cell_sem, k).wait()
        at = pl.ds(pl.multiple_of(k * chunk, chunk), chunk)
        s = dot_nt(k_pieces, cells[at].reshape(chunk * cols, width))
        one, two = [], []
        for i in range(chunk):
            x = s[:, i * cols : (i + 1) * cols]
            live = ids < counts[k * chunk + i]
            one.append(jnp.where(live, x[0:1] + x[1:2] + x[2:3], NEG_FILL))
            two.append(jnp.where(live, x[3:4] + x[4:5] + x[5:6], NEG_FILL))
        sr[at, :] = jnp.concatenate(one, 0)
        sc[at, :] = jnp.concatenate(two, 0)

    @pl.loop(1, half_n)
    def _(d):
        to_chips(lambda chip: chip_sum.at[chip], rs_buf.at[me_chip], s_rs, r_rs, d).wait_send()
        from_chips(lambda chip: rs_buf.at[chip], s_rs, r_rs, d).wait_recv()

    own = rs_buf[0]
    for i in range(1, half_n):
        own = own + rs_buf[i]
    cot_full[mine + me_chip] = own
    own_slot = cot_full.at[mine + me_chip]

    @pl.loop(1, half_n)
    def _(d):
        to_chips(lambda chip: own_slot, own_slot, s_ag, r_ag, d).start()


    score = sc[...]
    col_m = jnp.max(score, 0, keepdims=True)
    weight = jnp.where(score > 0.5 * NEG_FILL, jnp.exp(score - col_m), 0.0)
    wc[...] = weight
    col_t = jnp.sum(weight, 0, keepdims=True)
    for j, value in enumerate((col_m, col_t)):
        for i in range(q_rows):
            small[me_r, pl.ds(j * q_rows + i, 1), :] = value[:, i * 128 : (i + 1) * 128]
    small_x = (lambda peer: small.at[me_r], small, s_sm, r_sm)
    start_rows(*small_x)

    score = sr[...]
    row_m = jnp.max(score, 1, keepdims=True)
    row_weight = jnp.where(score > 0.5 * NEG_FILL, jnp.exp(score - row_m), 0.0)
    wr[...] = row_weight
    row_t = jnp.sum(row_weight, 1, keepdims=True)
    sub = lax.broadcasted_iota(jnp.int32, (chunk, 1), 0)

    @pl.loop(0, n_chunk)
    def _(k):
        at = pl.ds(pl.multiple_of(k * chunk, chunk), chunk)
        pieces = jnp.concatenate(split(wr[at, :], 2), 0).astype(BF16)
        acc = jnp.zeros((chunk, width), F32)
        for i in range(chunk):
            s = jnp.dot(pieces, cells[k * chunk + i], preferred_element_type=F32)
            acc = jnp.where(sub == i, s[0:chunk] + s[chunk : 2 * chunk], acc)
        row_pool[at, :] = acc

    row_buf[me_c, 0] = row_pool[...]
    row_buf[me_c, 1] = row_cot[...]
    row_buf[me_c, 2] = jnp.broadcast_to(row_m, (rows, width))
    row_buf[me_c, 3] = jnp.broadcast_to(row_t, (rows, width))
    row_x = (row_buf.at[me_c], row_buf, s_rx, r_rx)
    start_cols(*row_x)

    w_t = jnp.concatenate([p.T for p in split(weight, 2)], 1).astype(BF16)
    pick = lax.rem(lax.broadcasted_iota(jnp.int32, (2 * rows, 2 * width), 0), rows)
    lane = lax.broadcasted_iota(jnp.int32, (2 * rows, 2 * width), 1)
    pick = pick - jnp.where(lane < width, 0, 1)
    col_pool[...] = jnp.zeros_like(col_pool)

    @pl.loop(0, rows // 4)
    def _(k):
        acc = col_pool[...]
        for i in (0, 2):
            r = k * 4 + i
            one = jnp.where(pick == r, 1.0, 0.0).astype(BF16)
            spread = jnp.dot(w_t, one, preferred_element_type=F32)
            acc = acc + spread[:, :width] * cells[r].astype(F32)
            acc = acc + spread[:, width:] * cells[r + 1].astype(F32)
        col_pool[...] = acc

    wait_cols(*row_x)
    top = row_buf[0, 2]
    for i in range(1, n_col):
        top = jnp.maximum(top, row_buf[i, 2])
    pool = jnp.zeros((rows, width), F32)
    total = jnp.zeros((rows, width), F32)
    cot = jnp.zeros((rows, width), F32)
    for i in range(n_col):
        decay = jnp.exp(row_buf[i, 2] - top)
        pool = pool + row_buf[i, 0] * decay
        total = total + row_buf[i, 3] * decay
        cot = cot + row_buf[i, 1]
    factor = jnp.exp(row_buf[me_c, 2] - top) / total
    both = jnp.dot(wv_ref[...], wo_ref[...], preferred_element_type=F32)
    g_row = dot_nt(cot, both, HIGH)
    row_grad[...] = g_row
    row_dot = jnp.sum(pool * g_row, 1, keepdims=True) / total[:, 0:1]
    row_prob = wr[...] * factor[:, 0:1]

    @pl.loop(1, half_n)
    def _(d):
        to_chips(lambda chip: own_slot, own_slot, s_ag, r_ag, d).wait_send()
        from_chips(lambda chip: cot_full.at[mine + chip], s_ag, r_ag, d).wait_recv()

    half_at = cot_full.at[pl.ds(mine, half_n)]
    fill = to_sibling(half_at, half_at, s_pr.at[1], r_pr.at[1])
    fill.start()

    @pl.loop(0, n_chunk)
    def _(k):
        at = pl.ds(pl.multiple_of(k * chunk, chunk), chunk)
        pieces = jnp.concatenate(split(row_grad[at, :], 2), 0).astype(BF16)
        acc = jnp.zeros((chunk, cols), F32)
        for i in range(chunk):
            s = dot_nt(pieces, cells[k * chunk + i])
            acc = jnp.where(sub == i, s[0:chunk] + s[chunk : 2 * chunk], acc)
        rdp[at, :] = acc

    row_ds = row_prob * (rdp[...] - row_dot)
    sr[...] = row_ds

    wait_rows(*small_x)
    top = small[0, 0:q_rows]
    for i in range(1, n_row):
        top = jnp.maximum(top, small[i, 0:q_rows])
    total = jnp.zeros((q_rows, 128), F32)
    for i in range(n_row):
        total = total + small[i, q_rows : 2 * q_rows] * jnp.exp(small[i, 0:q_rows] - top)
    f_col = jnp.exp(col_m - flat_row(top)) / flat_row(total)
    col_prob = wc[...] * f_col
    wc[...] = col_prob
    f_t = jnp.broadcast_to(f_col, (8, cols)).T[:, 0:1]

    fill.wait_send()
    other_at = cot_full.at[pl.ds(other, half_n)]
    to_sibling(other_at, other_at, s_pr.at[1], r_pr.at[1]).wait_recv()
    cot_all = cot_full[...].reshape(cols, width)
    m_loc = dot_tn(col_pool[...] * f_t, cot_all, HIGH)
    m_loc = m_loc + dot_tn(row_pool[...] * factor, cot, HIGH)
    for i in range(n_row):
        red_src[i, 0:m_per] = m_loc[i * m_per : (i + 1) * m_per]
        if m_per < 8:
            red_src[i, m_per:8] = jnp.zeros((8 - m_per, width), F32)
    reduce = (lambda peer: red_src.at[peer], red_buf, s_rd, r_rd)
    start_rows(*reduce)
    red_buf[me_r] = red_src[me_r]

    g_col = dot_nt(cot_all, both, HIGH)
    g_out[...] = g_col

    @pl.loop(0, n_chunk)
    def _(k):
        at = pl.ds(pl.multiple_of(k * chunk, chunk), chunk)
        acc = jnp.zeros((16, cols), F32)
        for i in range(chunk):
            prod = cells[k * chunk + i].astype(F32) * g_out[...]
            hi = prod.astype(BF16)
            lo = (prod - hi.astype(F32)).astype(BF16)
            ones = jnp.where(sub16 == i, 1.0, 0.0).astype(BF16)
            acc = acc + dot_nt(ones, jnp.concatenate([hi, lo], 1))
        cdp[at, :] = acc[0:chunk]

    part_dot = jnp.sum(wc[...] * cdp[...], 0, keepdims=True)
    for i in range(q_rows):
        dots_buf[me_r, pl.ds(i, 1), :] = part_dot[:, i * 128 : (i + 1) * 128]
    dots_x = (lambda peer: dots_buf.at[me_r], dots_buf, s_dt, r_dt)
    start_rows(*dots_x)

    wait_rows(*reduce)
    acc = red_buf[0]
    for i in range(1, n_row):
        acc = acc + red_buf[i]
    part[me_c] = acc
    col_x = (part.at[me_c], part, s_cx, r_cx)
    start_cols(*col_x)

    wait_rows(*dots_x)
    dots = dots_buf[0, 0:q_rows]
    for i in range(1, n_row):
        dots = dots + dots_buf[i, 0:q_rows]
    col_ds = wc[...] * (cdp[...] - flat_row(dots))
    sc[...] = col_ds

    turn = lax.rem(lax.broadcasted_iota(jnp.int32, (4 * chunk, 1), 0), chunk)

    def moments(k, acc):
        at = pl.ds(pl.multiple_of(k * chunk, chunk), chunk)
        pieces = split(sr[at, :], 2) + split(sc[at, :], 2)
        pieces = jnp.concatenate(pieces, 0).astype(BF16)
        for i in range(chunk):
            s = jnp.dot(pieces, cells[k * chunk + i], preferred_element_type=F32)
            acc = acc + jnp.where(turn == i, s, 0.0)
        return acc

    acc = lax.fori_loop(0, n_chunk, moments, jnp.zeros((4 * chunk, width), F32))
    ab_buf[me_r] = jnp.concatenate(
        [
            jnp.sum(acc[0 : 2 * chunk], 0, keepdims=True),
            jnp.sum(acc[2 * chunk : 4 * chunk], 0, keepdims=True),
            jnp.zeros((6, width), F32),
        ],
        0,
    )
    ab_x = (lambda peer: ab_buf.at[me_r], ab_buf, s_ab, r_ab)
    start_rows(*ab_x)

    wait_cols(*col_x)
    acc = part[0]
    for i in range(1, n_col):
        acc = acc + part[i]
    m_full[me_r] = acc
    collect = (lambda peer: m_full.at[me_r], m_full, s_mg, r_mg)
    start_rows(*collect)

    pieces = [split(x, 2) for x in (row_prob, row_ds, col_ds, wc[...])]
    for half in range(2):
        block = jnp.concatenate([p[half] for p in pieces], 0)
        lhs_out[:, half * 4 * rows : (half + 1) * 4 * rows] = block.T.astype(BF16)
    zero = jnp.zeros((rows, width), F32)
    one = jnp.ones((rows, width), F32)
    left = jnp.concatenate(
        [g_row, jnp.broadcast_to(kr, (rows, width)), jnp.broadcast_to(kc, (rows, width)), zero], 0
    )
    right = jnp.concatenate([zero, zero, zero, one], 0)
    half = jnp.concatenate([left, right], 1)
    base_out[...] = jnp.concatenate([half, half], 0)

    owner = lax.rem(lax.broadcasted_iota(jnp.int32, base_out.shape, 0), rows)

    def write(k):
        at = pl.ds(k * chunk, chunk)
        return pltpu.make_async_copy(up.at[at], raw_hbm.at[at], out_sem.at[k])

    def cell_grads(first, last):
        @pl.loop(first, last)
        def _(k):
            for i in range(chunk):
                r = k * chunk + i
                rhs = jnp.where(owner == r, base_out[...], 0.0).astype(BF16)
                res = jnp.dot(lhs_out[...], rhs, preferred_element_type=F32)
                delta = res[:, :width] + res[:, width:] * g_out[...]
                up[r] = (up[r].astype(F32) + delta).astype(BF16)
            write(k).start()

    cell_grads(0, n_chunk // 2)

    wait_rows(*ab_x)
    acc = ab_buf[0]
    for i in range(1, n_row):
        acc = acc + ab_buf[i]
    ab_part[me_c] = acc
    ab_cx = (ab_part.at[me_c], ab_part, s_ac, r_ac)
    start_cols(*ab_cx)
    cell_grads(n_chunk // 2, n_chunk)
    wait_rows(*collect)
    m_out[...] = jnp.concatenate([m_full[i, 0:m_per] for i in range(n_row)], 0)
    wait_cols(*ab_cx)
    acc = ab_part[0]
    for i in range(1, n_col):
        acc = acc + ab_part[i]
    ab_out[...] = acc
    for k in range(n_chunk):
        write(k).wait()


def finish_kernel(
    pieces, raw_hbm, m_ref, ab_ref, wk_ref, wv_ref, wo_ref, rq_ref, cq_ref,
    out_hbm, kwg_ref, vwg_ref, owg_ref, rqg_ref, cqg_ref, stage, in_sem, out_sem,
):
    size = raw_hbm.shape[0] // pieces
    width = m_ref.shape[0]
    scale = 1.0 / math.sqrt(width)
    pairs = []
    for i in range(pieces):
        at = pl.ds(i * size, size)
        pairs.append(
            (
                pltpu.make_async_copy(raw_hbm.at[at], stage.at[at], in_sem.at[i]),
                pltpu.make_async_copy(stage.at[at], out_hbm.at[at], out_sem.at[i]),
            )
        )
    for load, _ in pairs:
        load.start()
    for load, store in pairs:
        load.wait()
        store.start()
    ab, m = ab_ref[...], m_ref[...]
    queries = jnp.concatenate([rq_ref[...], cq_ref[...], jnp.zeros((6, width), F32)], 0)
    kwg_ref[...] = dot_tn(ab, queries * scale, HIGH)
    q_grad = dot_nn(ab, wk_ref[...].astype(F32), HIGH) * scale
    rqg_ref[...] = q_grad[0:1]
    cqg_ref[...] = q_grad[1:2]
    vwg_ref[...] = dot_nt(m, wo_ref[...].astype(F32), HIGH)
    owg_ref[...] = dot_tn(wv_ref[...].astype(F32), m, HIGH)
    for _, store in pairs:
        store.wait()


def on_device(n_row, n_col, cells, upstream, counts, wk, wv, wo, rq, cq):
    rows, cols, width = cells.shape
    chunk = 8
    per = cols // n_row
    rq, cq = rq.reshape(1, width), cq.reshape(1, width)
    vmem = pl.BlockSpec(memory_space=pltpu.VMEM)
    hbm = pl.BlockSpec(memory_space=pl.ANY)
    n_chunk = rows // chunk
    dma = pltpu.SemaphoreType.DMA
    f32 = lambda *shape: pltpu.VMEM(shape, F32)
    small_rows = -(-2 * (cols // 128) // 8) * 8
    dots_rows = -(-(cols // 128) // 8) * 8
    square = jax.ShapeDtypeStruct((width, width), F32)
    vector = jax.ShapeDtypeStruct((1, width), F32)
    half_n = n_row // 2
    over_row, over_col, over_chip = dma((n_row,)), dma((n_col,)), dma((half_n,))
    raw, m, ab = pl.pallas_call(
        functools.partial(stats_kernel, n_row, n_col, chunk),
        out_shape=(
            jax.ShapeDtypeStruct(cells.shape, BF16),
            square,
            jax.ShapeDtypeStruct((8, width), F32),
        ),
        in_specs=[hbm, hbm, pl.BlockSpec(memory_space=pltpu.SMEM)] + [hbm] * 5,
        out_specs=(hbm, vmem, vmem),
        scratch_shapes=[
            pltpu.VMEM((cols, 8 * rows), BF16), f32(8 * rows, 2 * width), f32(cols, width),
            pltpu.VMEM(cells.shape, BF16), pltpu.VMEM(cells.shape, BF16),
            f32(n_row, per, width), f32(half_n, per, width), f32(half_n, per, width),
            f32(half_n, per, width), f32(n_row, per, width),
            f32(rows, width),
            f32(rows, cols), f32(rows, cols), f32(rows, cols), f32(rows, cols),
            f32(rows, cols), f32(rows, cols),
            f32(rows, width), f32(rows, width), f32(cols, width),
            f32(n_col, 4, rows, width),
            f32(n_row, small_rows, 128), f32(n_row, dots_rows, 128),
            f32(n_row, 8, width), f32(n_row, 8, width), f32(n_col, 8, width),
            f32(n_row, 8, width),
            f32(n_row, 8, width), f32(n_col, 8, width),
            pltpu.VMEM(wk.shape, BF16), pltpu.VMEM(wv.shape, BF16), pltpu.VMEM(wo.shape, BF16),
            f32(1, width), f32(1, width),
            dma((n_chunk,)), dma((n_chunk,)), dma((5,)), dma((n_chunk,)),
            dma((2,)), dma((2,)),
            over_chip, over_chip, over_chip, over_chip,
            over_col, over_col, over_row, over_row, over_row, over_row,
            over_row, over_row, over_col, over_col, over_row, over_row,
            over_row, over_row, over_col, over_col,
        ],
        compiler_params=pltpu.CompilerParams(
            collective_id=0, has_side_effects=True, vmem_limit_bytes=VMEM_BYTES
        ),
        name="hub_stats",
    )(cells, upstream, counts, wk, wv, wo, rq, cq)
    pieces = 8
    cell_grad, kwg, vwg, owg, rqg, cqg = pl.pallas_call(
        functools.partial(finish_kernel, pieces),
        out_shape=(
            jax.ShapeDtypeStruct(cells.shape, cells.dtype),
            square, square, square, vector, vector,
        ),
        in_specs=[hbm] + [vmem] * 7,
        out_specs=(hbm,) + (vmem,) * 5,
        scratch_shapes=[pltpu.VMEM(cells.shape, BF16), dma((pieces,)), dma((pieces,))],
        compiler_params=pltpu.CompilerParams(vmem_limit_bytes=VMEM_BYTES),
        name="finish",
    )(raw, m, ab, wk, wv, wo, rq, cq)
    return cell_grad, kwg, vwg, owg, rqg.reshape(width), cqg.reshape(width)


def solution(mesh):
    placed = (P("row", "col", None), P("row", "col", None), P("row"), P(), P(), P(), P(), P())
    return jax.shard_map(
        functools.partial(on_device, mesh.shape["row"], mesh.shape["col"]),
        mesh=mesh,
        in_specs=placed,
        out_specs=(P("row", "col", None), P(), P(), P(), P(), P()),
        check_vma=False,
    )
```

```python
import functools
import math

import jax
import jax.numpy as jnp
from jax import lax
from jax.experimental import pallas as pl
from jax.experimental.pallas import tpu as pltpu
from jax.sharding import PartitionSpec as P

NEG_FILL = -1e30
HIGH = lax.Precision.HIGHEST
MESH = pl.DeviceIdType.MESH
F32 = jnp.float32
BF16 = jnp.bfloat16
VMEM_BYTES = 62 * 1024 * 1024


def dot_nt(a, b, precision=None):
    return lax.dot_general(
        a, b, (((1,), (1,)), ((), ())), precision=precision, preferred_element_type=F32
    )


def dot_tn(a, b, precision=None):
    return lax.dot_general(
        a, b, (((0,), (0,)), ((), ())), precision=precision, preferred_element_type=F32
    )


def dot_nn(a, b, precision=None):
    return jnp.dot(a, b, precision=precision, preferred_element_type=F32)


def split(x, parts):
    pieces = []
    for _ in range(parts):
        piece = x.astype(BF16).astype(F32)
        pieces.append(piece)
        x = x - piece
    return pieces


def stack_rows(rows, width):
    pad = jnp.zeros((16 - len(rows), width), F32)
    return jnp.concatenate(rows + [pad], 0).astype(BF16)


def flat_row(tile):
    return jnp.concatenate([tile[i : i + 1] for i in range(tile.shape[0])], 1)


def stats_kernel(
    n_row, n_col, chunk,
    cells_hbm, up_hbm, counts, wk_hbm, wv_hbm, wo_hbm, rq_hbm, cq_hbm,
    raw_hbm, m_out, ab_out,
    lhs_out, base_out, g_out,
    cells, up, cot_loc, pair_buf, chip_sum, rs_buf, cot_full, row_cot, sr, sc, wr, wc, rdp, cdp,
    row_pool, row_grad, col_pool, row_buf, small, dots_buf, red_src, red_buf, part, m_full,
    ab_buf, ab_part, wk_ref, wv_ref, wo_ref, rq_ref, cq_ref,
    cell_sem, up_sem, in_sem, out_sem, s_pr, r_pr, s_rs, r_rs, s_ag, r_ag, s_rx, r_rx, s_sm, r_sm, s_dt, r_dt,
    s_rd, r_rd, s_cx, r_cx, s_mg, r_mg, s_ab, r_ab, s_ac, r_ac,
):
    rows, cols, width = cells.shape
    scale = 1.0 / math.sqrt(width)
    me_r = lax.axis_index("row")
    me_c = lax.axis_index("col")
    n_chunk = rows // chunk
    per = cols // n_row
    m_per = width // n_row
    q_rows = cols // 128

    def local(hbm, vmem, sem, k):
        return pltpu.make_async_copy(
            hbm.at[pl.ds(k * chunk, chunk)], vmem.at[pl.ds(k * chunk, chunk)], sem.at[k]
        )

    for k in range(n_chunk):
        local(up_hbm, up, up_sem, k).start()
    small_in = [
        pltpu.make_async_copy(src, dst, in_sem.at[i])
        for i, (src, dst) in enumerate(
            ((wk_hbm, wk_ref), (wv_hbm, wv_ref), (wo_hbm, wo_ref), (rq_hbm, rq_ref), (cq_hbm, cq_ref))
        )
    ]
    for copy in small_in:
        copy.start()
    for k in range(n_chunk):
        local(cells_hbm, cells, cell_sem, k).start()
    sub16 = lax.broadcasted_iota(jnp.int32, (16, 2 * width), 0)

    barrier = pltpu.get_barrier_semaphore()

    @pl.loop(1, n_row)
    def _(d):
        pl.semaphore_signal(
            barrier, inc=1, device_id=(lax.rem(me_r + d, n_row), me_c), device_id_type=MESH
        )

    @pl.loop(1, n_col)
    def _(d):
        pl.semaphore_signal(
            barrier, inc=1, device_id=(me_r, lax.rem(me_c + d, n_col)), device_id_type=MESH
        )

    def to_rows(src_of, dst, s_sem, r_sem, d):
        peer = lax.rem(me_r + d, n_row)
        return pltpu.make_async_remote_copy(
            src_ref=src_of(peer), dst_ref=dst.at[me_r], send_sem=s_sem.at[d],
            recv_sem=r_sem.at[d], device_id=(peer, me_c), device_id_type=MESH,
        )

    def from_rows(src_of, dst, s_sem, r_sem, d):
        peer = lax.rem(me_r + n_row - d, n_row)
        return pltpu.make_async_remote_copy(
            src_ref=src_of(peer), dst_ref=dst.at[peer], send_sem=s_sem.at[d],
            recv_sem=r_sem.at[d], device_id=(peer, me_c), device_id_type=MESH,
        )

    def to_cols(src, dst, s_sem, r_sem, d):
        peer = lax.rem(me_c + d, n_col)
        return pltpu.make_async_remote_copy(
            src_ref=src, dst_ref=dst.at[me_c], send_sem=s_sem.at[d],
            recv_sem=r_sem.at[d], device_id=(me_r, peer), device_id_type=MESH,
        )

    def from_cols(src, dst, s_sem, r_sem, d):
        peer = lax.rem(me_c + n_col - d, n_col)
        return pltpu.make_async_remote_copy(
            src_ref=src, dst_ref=dst.at[peer], send_sem=s_sem.at[d],
            recv_sem=r_sem.at[d], device_id=(me_r, peer), device_id_type=MESH,
        )

    half_n = n_row // 2
    me_core, me_chip = lax.rem(me_r, 2), lax.div(me_r, 2)
    mine, other = me_core * half_n, (1 - me_core) * half_n

    def to_sibling(src, dst, s_sem, r_sem):
        return pltpu.make_async_remote_copy(
            src_ref=src, dst_ref=dst, send_sem=s_sem, recv_sem=r_sem,
            device_id=(me_r + 1 - 2 * me_core, me_c), device_id_type=MESH,
        )

    def to_chips(src_of, dst, s_sem, r_sem, d):
        chip = lax.rem(me_chip + d, half_n)
        return pltpu.make_async_remote_copy(
            src_ref=src_of(chip), dst_ref=dst, send_sem=s_sem.at[d], recv_sem=r_sem.at[d],
            device_id=(chip * 2 + me_core, me_c), device_id_type=MESH,
        )

    def from_chips(dst_of, s_sem, r_sem, d):
        chip = lax.rem(me_chip + half_n - d, half_n)
        return pltpu.make_async_remote_copy(
            src_ref=dst_of(chip), dst_ref=dst_of(chip), send_sem=s_sem.at[d],
            recv_sem=r_sem.at[d], device_id=(chip * 2 + me_core, me_c), device_id_type=MESH,
        )

    def start_rows(*args):
        @pl.loop(1, n_row)
        def _(d):
            to_rows(*args, d).start()

    def wait_rows(*args):
        @pl.loop(1, n_row)
        def _(d):
            to_rows(*args, d).wait_send()
            from_rows(*args, d).wait_recv()

    def start_cols(*args):
        @pl.loop(1, n_col)
        def _(d):
            to_cols(*args, d).start()

    def wait_cols(*args):
        @pl.loop(1, n_col)
        def _(d):
            to_cols(*args, d).wait_send()
            from_cols(*args, d).wait_recv()

    span = 64
    groups = span // per
    for k in range(n_chunk):
        local(up_hbm, up, up_sem, k).wait()

        def add_block(cb, total, k=k):
            x = up[pl.ds(k * chunk, chunk), pl.ds(pl.multiple_of(cb * span, span), span), :]
            x = x.astype(F32)
            by_col = jnp.sum(x, 0).reshape(groups, per, width)
            at = pl.ds(cb * groups, groups)
            cot_loc[at] = by_col if k == 0 else cot_loc[at] + by_col
            return total + jnp.sum(x, 1)

        row_cot[pl.ds(k * chunk, chunk), :] = lax.fori_loop(
            0, cols // span, add_block, jnp.zeros((chunk, width), F32)
        )

    pl.semaphore_wait(barrier, n_row + n_col - 2)
    swap = to_sibling(cot_loc.at[pl.ds(other, half_n)], pair_buf, s_pr.at[0], r_pr.at[0])
    swap.start()

    for copy in small_in:
        copy.wait()
    wk = wk_ref[...].astype(F32)
    queries = jnp.concatenate([rq_ref[...], cq_ref[...], jnp.zeros((6, width), F32)], 0)
    kvec = dot_nt(queries, wk, HIGH) * scale
    kr, kc = kvec[0:1], kvec[1:2]
    k_pieces = stack_rows(split(kr, 3) + split(kc, 3), width)
    ids = me_c * cols + lax.broadcasted_iota(jnp.int32, (1, cols), 1)

    swap.wait()
    chip_sum[...] = cot_loc[pl.ds(mine, half_n)] + pair_buf[...]
    rs_buf[me_chip] = chip_sum[me_chip]

    @pl.loop(1, half_n)
    def _(d):
        to_chips(lambda chip: chip_sum.at[chip], rs_buf.at[me_chip], s_rs, r_rs, d).start()

    @pl.loop(0, n_chunk)
    def _(k):
        local(cells_hbm, cells, cell_sem, k).wait()
        at = pl.ds(pl.multiple_of(k * chunk, chunk), chunk)
        s = dot_nt(k_pieces, cells[at].reshape(chunk * cols, width))
        one, two = [], []
        for i in range(chunk):
            x = s[:, i * cols : (i + 1) * cols]
            live = ids < counts[k * chunk + i]
            one.append(jnp.where(live, x[0:1] + x[1:2] + x[2:3], NEG_FILL))
            two.append(jnp.where(live, x[3:4] + x[4:5] + x[5:6], NEG_FILL))
        sr[at, :] = jnp.concatenate(one, 0)
        sc[at, :] = jnp.concatenate(two, 0)

    @pl.loop(1, half_n)
    def _(d):
        to_chips(lambda chip: chip_sum.at[chip], rs_buf.at[me_chip], s_rs, r_rs, d).wait_send()
        from_chips(lambda chip: rs_buf.at[chip], s_rs, r_rs, d).wait_recv()

    own = rs_buf[0]
    for i in range(1, half_n):
        own = own + rs_buf[i]
    cot_full[mine + me_chip] = own
    own_slot = cot_full.at[mine + me_chip]

    @pl.loop(1, half_n)
    def _(d):
        to_chips(lambda chip: own_slot, own_slot, s_ag, r_ag, d).start()


    score = sc[...]
    col_m = jnp.max(score, 0, keepdims=True)
    weight = jnp.where(score > 0.5 * NEG_FILL, jnp.exp(score - col_m), 0.0)
    wc[...] = weight
    col_t = jnp.sum(weight, 0, keepdims=True)
    for j, value in enumerate((col_m, col_t)):
        for i in range(q_rows):
            small[me_r, pl.ds(j * q_rows + i, 1), :] = value[:, i * 128 : (i + 1) * 128]
    small_x = (lambda peer: small.at[me_r], small, s_sm, r_sm)
    start_rows(*small_x)

    score = sr[...]
    row_m = jnp.max(score, 1, keepdims=True)
    row_weight = jnp.where(score > 0.5 * NEG_FILL, jnp.exp(score - row_m), 0.0)
    wr[...] = row_weight
    row_t = jnp.sum(row_weight, 1, keepdims=True)
    sub = lax.broadcasted_iota(jnp.int32, (chunk, 1), 0)

    @pl.loop(0, n_chunk)
    def _(k):
        at = pl.ds(pl.multiple_of(k * chunk, chunk), chunk)
        pieces = jnp.concatenate(split(wr[at, :], 2), 0).astype(BF16)
        acc = jnp.zeros((chunk, width), F32)
        for i in range(chunk):
            s = jnp.dot(pieces, cells[k * chunk + i], preferred_element_type=F32)
            acc = jnp.where(sub == i, s[0:chunk] + s[chunk : 2 * chunk], acc)
        row_pool[at, :] = acc

    row_buf[me_c, 0] = row_pool[...]
    row_buf[me_c, 1] = row_cot[...]
    row_buf[me_c, 2] = jnp.broadcast_to(row_m, (rows, width))
    row_buf[me_c, 3] = jnp.broadcast_to(row_t, (rows, width))
    row_x = (row_buf.at[me_c], row_buf, s_rx, r_rx)
    start_cols(*row_x)

    w_t = jnp.concatenate([p.T for p in split(weight, 2)], 1).astype(BF16)
    pick = lax.rem(lax.broadcasted_iota(jnp.int32, (2 * rows, 2 * width), 0), rows)
    lane = lax.broadcasted_iota(jnp.int32, (2 * rows, 2 * width), 1)
    pick = pick - jnp.where(lane < width, 0, 1)
    col_pool[...] = jnp.zeros_like(col_pool)

    @pl.loop(0, rows // 4)
    def _(k):
        acc = col_pool[...]
        for i in (0, 2):
            r = k * 4 + i
            one = jnp.where(pick == r, 1.0, 0.0).astype(BF16)
            spread = jnp.dot(w_t, one, preferred_element_type=F32)
            acc = acc + spread[:, :width] * cells[r].astype(F32)
            acc = acc + spread[:, width:] * cells[r + 1].astype(F32)
        col_pool[...] = acc

    wait_cols(*row_x)
    top = row_buf[0, 2]
    for i in range(1, n_col):
        top = jnp.maximum(top, row_buf[i, 2])
    pool = jnp.zeros((rows, width), F32)
    total = jnp.zeros((rows, width), F32)
    cot = jnp.zeros((rows, width), F32)
    for i in range(n_col):
        decay = jnp.exp(row_buf[i, 2] - top)
        pool = pool + row_buf[i, 0] * decay
        total = total + row_buf[i, 3] * decay
        cot = cot + row_buf[i, 1]
    factor = jnp.exp(row_buf[me_c, 2] - top) / total
    both = jnp.dot(wv_ref[...], wo_ref[...], preferred_element_type=F32)
    g_row = dot_nt(cot, both, HIGH)
    row_grad[...] = g_row
    row_dot = jnp.sum(pool * g_row, 1, keepdims=True) / total[:, 0:1]
    row_prob = wr[...] * factor[:, 0:1]

    @pl.loop(1, half_n)
    def _(d):
        to_chips(lambda chip: own_slot, own_slot, s_ag, r_ag, d).wait_send()
        from_chips(lambda chip: cot_full.at[mine + chip], s_ag, r_ag, d).wait_recv()

    half_at = cot_full.at[pl.ds(mine, half_n)]
    fill = to_sibling(half_at, half_at, s_pr.at[1], r_pr.at[1])
    fill.start()

    @pl.loop(0, n_chunk)
    def _(k):
        at = pl.ds(pl.multiple_of(k * chunk, chunk), chunk)
        pieces = jnp.concatenate(split(row_grad[at, :], 2), 0).astype(BF16)
        acc = jnp.zeros((chunk, cols), F32)
        for i in range(chunk):
            s = dot_nt(pieces, cells[k * chunk + i])
            acc = jnp.where(sub == i, s[0:chunk] + s[chunk : 2 * chunk], acc)
        rdp[at, :] = acc

    row_ds = row_prob * (rdp[...] - row_dot)
    sr[...] = row_ds

    wait_rows(*small_x)
    top = small[0, 0:q_rows]
    for i in range(1, n_row):
        top = jnp.maximum(top, small[i, 0:q_rows])
    total = jnp.zeros((q_rows, 128), F32)
    for i in range(n_row):
        total = total + small[i, q_rows : 2 * q_rows] * jnp.exp(small[i, 0:q_rows] - top)
    f_col = jnp.exp(col_m - flat_row(top)) / flat_row(total)
    col_prob = wc[...] * f_col
    wc[...] = col_prob
    f_t = jnp.broadcast_to(f_col, (8, cols)).T[:, 0:1]

    fill.wait_send()
    other_at = cot_full.at[pl.ds(other, half_n)]
    to_sibling(other_at, other_at, s_pr.at[1], r_pr.at[1]).wait_recv()
    cot_all = cot_full[...].reshape(cols, width)
    g_col = dot_nt(cot_all, both, HIGH)
    g_out[...] = g_col

    @pl.loop(0, n_chunk)
    def _(k):
        at = pl.ds(pl.multiple_of(k * chunk, chunk), chunk)
        acc = jnp.zeros((16, cols), F32)
        for i in range(chunk):
            prod = cells[k * chunk + i].astype(F32) * g_out[...]
            hi = prod.astype(BF16)
            lo = (prod - hi.astype(F32)).astype(BF16)
            ones = jnp.where(sub16 == i, 1.0, 0.0).astype(BF16)
            acc = acc + dot_nt(ones, jnp.concatenate([hi, lo], 1))
        cdp[at, :] = acc[0:chunk]

    part_dot = jnp.sum(wc[...] * cdp[...], 0, keepdims=True)
    for i in range(q_rows):
        dots_buf[me_r, pl.ds(i, 1), :] = part_dot[:, i * 128 : (i + 1) * 128]
    dots_x = (lambda peer: dots_buf.at[me_r], dots_buf, s_dt, r_dt)
    start_rows(*dots_x)

    m_loc = dot_tn(col_pool[...] * f_t, cot_all, HIGH)
    m_loc = m_loc + dot_tn(row_pool[...] * factor, cot, HIGH)
    for i in range(n_row):
        red_src[i, 0:m_per] = m_loc[i * m_per : (i + 1) * m_per]
        if m_per < 8:
            red_src[i, m_per:8] = jnp.zeros((8 - m_per, width), F32)
    reduce = (lambda peer: red_src.at[peer], red_buf, s_rd, r_rd)
    start_rows(*reduce)
    red_buf[me_r] = red_src[me_r]

    zero = jnp.zeros((rows, width), F32)
    one = jnp.ones((rows, width), F32)
    left = jnp.concatenate(
        [g_row, jnp.broadcast_to(kr, (rows, width)), jnp.broadcast_to(kc, (rows, width)), zero], 0
    )
    right = jnp.concatenate([zero, zero, zero, one], 0)
    half = jnp.concatenate([left, right], 1)
    base_out[...] = jnp.concatenate([half, half], 0)

    wait_rows(*dots_x)
    dots = dots_buf[0, 0:q_rows]
    for i in range(1, n_row):
        dots = dots + dots_buf[i, 0:q_rows]
    col_ds = wc[...] * (cdp[...] - flat_row(dots))
    sc[...] = col_ds

    turn = lax.rem(lax.broadcasted_iota(jnp.int32, (4 * chunk, 1), 0), chunk)

    def moments(k, acc):
        at = pl.ds(pl.multiple_of(k * chunk, chunk), chunk)
        pieces = split(sr[at, :], 2) + split(sc[at, :], 2)
        pieces = jnp.concatenate(pieces, 0).astype(BF16)
        for i in range(chunk):
            s = jnp.dot(pieces, cells[k * chunk + i], preferred_element_type=F32)
            acc = acc + jnp.where(turn == i, s, 0.0)
        return acc

    acc = lax.fori_loop(0, n_chunk, moments, jnp.zeros((4 * chunk, width), F32))
    ab_buf[me_r] = jnp.concatenate(
        [
            jnp.sum(acc[0 : 2 * chunk], 0, keepdims=True),
            jnp.sum(acc[2 * chunk : 4 * chunk], 0, keepdims=True),
            jnp.zeros((6, width), F32),
        ],
        0,
    )
    ab_x = (lambda peer: ab_buf.at[me_r], ab_buf, s_ab, r_ab)
    start_rows(*ab_x)

    wait_rows(*reduce)
    acc = red_buf[0]
    for i in range(1, n_row):
        acc = acc + red_buf[i]
    part[me_c] = acc
    col_x = (part.at[me_c], part, s_cx, r_cx)
    start_cols(*col_x)

    pieces = [split(x, 2) for x in (row_prob, row_ds, col_ds, wc[...])]
    for half in range(2):
        block = jnp.concatenate([p[half] for p in pieces], 0)
        lhs_out[:, half * 4 * rows : (half + 1) * 4 * rows] = block.T.astype(BF16)
    owner = lax.rem(lax.broadcasted_iota(jnp.int32, base_out.shape, 0), rows)

    def write(k):
        at = pl.ds(k * chunk, chunk)
        return pltpu.make_async_copy(up.at[at], raw_hbm.at[at], out_sem.at[k])

    def cell_grads(first, last):
        @pl.loop(first, last)
        def _(k):
            for i in range(chunk):
                r = k * chunk + i
                rhs = jnp.where(owner == r, base_out[...], 0.0).astype(BF16)
                res = jnp.dot(lhs_out[...], rhs, preferred_element_type=F32)
                delta = res[:, :width] + res[:, width:] * g_out[...]
                up[r] = (up[r].astype(F32) + delta).astype(BF16)
            write(k).start()

    cell_grads(0, n_chunk // 4)
    wait_cols(*col_x)
    acc = part[0]
    for i in range(1, n_col):
        acc = acc + part[i]
    m_full[me_r] = acc
    collect = (lambda peer: m_full.at[me_r], m_full, s_mg, r_mg)
    start_rows(*collect)
    cell_grads(n_chunk // 4, n_chunk // 2)

    wait_rows(*ab_x)
    acc = ab_buf[0]
    for i in range(1, n_row):
        acc = acc + ab_buf[i]
    ab_part[me_c] = acc
    ab_cx = (ab_part.at[me_c], ab_part, s_ac, r_ac)
    start_cols(*ab_cx)
    cell_grads(n_chunk // 2, n_chunk)
    wait_rows(*collect)
    m_out[...] = jnp.concatenate([m_full[i, 0:m_per] for i in range(n_row)], 0)
    wait_cols(*ab_cx)
    acc = ab_part[0]
    for i in range(1, n_col):
        acc = acc + ab_part[i]
    ab_out[...] = acc
    for k in range(n_chunk):
        write(k).wait()


def finish_kernel(
    pieces, raw_hbm, m_hbm, ab_hbm, wk_hbm, wv_hbm, wo_hbm, rq_hbm, cq_hbm,
    out_hbm, kwg_hbm, vwg_hbm, owg_hbm, rqg_hbm, cqg_hbm,
    stage, m_ref, ab_ref, wk_ref, wv_ref, wo_ref, rq_ref, cq_ref,
    kwg_ref, vwg_ref, owg_ref, rqg_ref, cqg_ref, in_sem, out_sem, arg_sem, res_sem,
):
    size = raw_hbm.shape[0] // pieces
    width = m_ref.shape[0]
    scale = 1.0 / math.sqrt(width)

    def copies(sources, targets, sem):
        return [
            pltpu.make_async_copy(src, dst, sem.at[i])
            for i, (src, dst) in enumerate(zip(sources, targets))
        ]

    arguments = copies(
        (m_hbm, ab_hbm, wk_hbm, wv_hbm, wo_hbm, rq_hbm, cq_hbm),
        (m_ref, ab_ref, wk_ref, wv_ref, wo_ref, rq_ref, cq_ref),
        arg_sem,
    )
    results = copies(
        (kwg_ref, vwg_ref, owg_ref, rqg_ref, cqg_ref),
        (kwg_hbm, vwg_hbm, owg_hbm, rqg_hbm, cqg_hbm),
        res_sem,
    )
    parts = [pl.ds(i * size, size) for i in range(pieces)]
    loads = copies([raw_hbm.at[p] for p in parts], [stage.at[p] for p in parts], in_sem)
    stores = copies([stage.at[p] for p in parts], [out_hbm.at[p] for p in parts], out_sem)
    for copy in arguments + loads:
        copy.start()

    def forward(first, last):
        for i in range(first, last):
            loads[i].wait()
            stores[i].start()

    for copy in arguments:
        copy.wait()
    forward(0, pieces // 4)
    ab, m = ab_ref[...], m_ref[...]
    queries = jnp.concatenate([rq_ref[...], cq_ref[...], jnp.zeros((6, width), F32)], 0)
    kwg_ref[...] = dot_tn(ab, queries * scale, HIGH)
    q_grad = dot_nn(ab, wk_ref[...].astype(F32), HIGH) * scale
    rqg_ref[...] = q_grad[0:1]
    cqg_ref[...] = q_grad[1:2]
    forward(pieces // 4, pieces // 2)
    vwg_ref[...] = dot_nt(m, wo_ref[...].astype(F32), HIGH)
    forward(pieces // 2, pieces)
    owg_ref[...] = dot_tn(wv_ref[...].astype(F32), m, HIGH)
    for copy in results:
        copy.start()
    for copy in stores + results:
        copy.wait()


def on_device(n_row, n_col, cells, upstream, counts, wk, wv, wo, rq, cq):
    rows, cols, width = cells.shape
    chunk = 8
    per = cols // n_row
    rq, cq = rq.reshape(1, width), cq.reshape(1, width)
    vmem = pl.BlockSpec(memory_space=pltpu.VMEM)
    hbm = pl.BlockSpec(memory_space=pl.ANY)
    n_chunk = rows // chunk
    dma = pltpu.SemaphoreType.DMA
    f32 = lambda *shape: pltpu.VMEM(shape, F32)
    small_rows = -(-2 * (cols // 128) // 8) * 8
    dots_rows = -(-(cols // 128) // 8) * 8
    square = jax.ShapeDtypeStruct((width, width), F32)
    vector = jax.ShapeDtypeStruct((1, width), F32)
    half_n = n_row // 2
    over_row, over_col, over_chip = dma((n_row,)), dma((n_col,)), dma((half_n,))
    raw, m, ab = pl.pallas_call(
        functools.partial(stats_kernel, n_row, n_col, chunk),
        out_shape=(
            jax.ShapeDtypeStruct(cells.shape, BF16),
            square,
            jax.ShapeDtypeStruct((8, width), F32),
        ),
        in_specs=[hbm, hbm, pl.BlockSpec(memory_space=pltpu.SMEM)] + [hbm] * 5,
        out_specs=(hbm, vmem, vmem),
        scratch_shapes=[
            pltpu.VMEM((cols, 8 * rows), BF16), f32(8 * rows, 2 * width), f32(cols, width),
            pltpu.VMEM(cells.shape, BF16), pltpu.VMEM(cells.shape, BF16),
            f32(n_row, per, width), f32(half_n, per, width), f32(half_n, per, width),
            f32(half_n, per, width), f32(n_row, per, width),
            f32(rows, width),
            f32(rows, cols), f32(rows, cols), f32(rows, cols), f32(rows, cols),
            f32(rows, cols), f32(rows, cols),
            f32(rows, width), f32(rows, width), f32(cols, width),
            f32(n_col, 4, rows, width),
            f32(n_row, small_rows, 128), f32(n_row, dots_rows, 128),
            f32(n_row, 8, width), f32(n_row, 8, width), f32(n_col, 8, width),
            f32(n_row, 8, width),
            f32(n_row, 8, width), f32(n_col, 8, width),
            pltpu.VMEM(wk.shape, BF16), pltpu.VMEM(wv.shape, BF16), pltpu.VMEM(wo.shape, BF16),
            f32(1, width), f32(1, width),
            dma((n_chunk,)), dma((n_chunk,)), dma((5,)), dma((n_chunk,)),
            dma((2,)), dma((2,)),
            over_chip, over_chip, over_chip, over_chip,
            over_col, over_col, over_row, over_row, over_row, over_row,
            over_row, over_row, over_col, over_col, over_row, over_row,
            over_row, over_row, over_col, over_col,
        ],
        compiler_params=pltpu.CompilerParams(
            collective_id=0, has_side_effects=True, vmem_limit_bytes=VMEM_BYTES
        ),
        name="hub_stats",
    )(cells, upstream, counts, wk, wv, wo, rq, cq)
    pieces = 8
    cell_grad, kwg, vwg, owg, rqg, cqg = pl.pallas_call(
        functools.partial(finish_kernel, pieces),
        out_shape=(
            jax.ShapeDtypeStruct(cells.shape, cells.dtype),
            square, square, square, vector, vector,
        ),
        in_specs=[hbm] * 8,
        out_specs=(hbm,) * 6,
        scratch_shapes=[
            pltpu.VMEM(cells.shape, BF16), f32(width, width), f32(8, width),
            pltpu.VMEM(wk.shape, BF16), pltpu.VMEM(wv.shape, BF16), pltpu.VMEM(wo.shape, BF16),
            f32(1, width), f32(1, width),
            f32(width, width), f32(width, width), f32(width, width), f32(1, width), f32(1, width),
            dma((pieces,)), dma((pieces,)), dma((7,)), dma((5,)),
        ],
        compiler_params=pltpu.CompilerParams(vmem_limit_bytes=VMEM_BYTES),
        name="finish",
    )(raw, m, ab, wk, wv, wo, rq, cq)
    return cell_grad, kwg, vwg, owg, rqg.reshape(width), cqg.reshape(width)


def solution(mesh):
    placed = (P("row", "col", None), P("row", "col", None), P("row"), P(), P(), P(), P(), P())
    return jax.shard_map(
        functools.partial(on_device, mesh.shape["row"], mesh.shape["col"]),
        mesh=mesh,
        in_specs=placed,
        out_specs=(P("row", "col", None), P(), P(), P(), P(), P()),
        check_vma=False,
    )
```

```python
import functools
import math

import jax
import jax.numpy as jnp
from jax import lax
from jax.experimental import pallas as pl
from jax.experimental.pallas import tpu as pltpu
from jax.sharding import PartitionSpec as P

NEG_FILL = -1e30
HIGH = lax.Precision.HIGHEST
MESH = pl.DeviceIdType.MESH
F32 = jnp.float32
BF16 = jnp.bfloat16
VMEM_BYTES = 62 * 1024 * 1024


def dot_nt(a, b, precision=None):
    return lax.dot_general(
        a, b, (((1,), (1,)), ((), ())), precision=precision, preferred_element_type=F32
    )


def dot_tn(a, b, precision=None):
    return lax.dot_general(
        a, b, (((0,), (0,)), ((), ())), precision=precision, preferred_element_type=F32
    )


def dot_nn(a, b, precision=None):
    return jnp.dot(a, b, precision=precision, preferred_element_type=F32)


def split(x, parts):
    pieces = []
    for _ in range(parts):
        piece = x.astype(BF16).astype(F32)
        pieces.append(piece)
        x = x - piece
    return pieces


def stack_rows(rows, width):
    pad = jnp.zeros((16 - len(rows), width), F32)
    return jnp.concatenate(rows + [pad], 0).astype(BF16)


def flat_row(tile):
    return jnp.concatenate([tile[i : i + 1] for i in range(tile.shape[0])], 1)


def stats_kernel(
    n_row, n_col, chunk,
    cells_hbm, up_hbm, counts, wk_hbm, wv_hbm, wo_hbm, rq_hbm, cq_hbm,
    raw_hbm, m_out, ab_out,
    lhs_out, base_out, g_out,
    cells, up, cot_loc, pair_buf, chip_sum, rs_buf, cot_full, row_cot, sr, sc, wr, wc, rdp, cdp,
    row_pool, row_grad, col_pool, row_buf, small, dots_buf, red_src, red_buf, part, m_full,
    ab_buf, ab_part, wk_ref, wv_ref, wo_ref, rq_ref, cq_ref,
    cell_sem, up_sem, in_sem, out_sem, s_pr, r_pr, s_rs, r_rs, s_ag, r_ag, s_rx, r_rx, s_sm, r_sm, s_dt, r_dt,
    s_rd, r_rd, s_cx, r_cx, s_mg, r_mg, s_ab, r_ab, s_ac, r_ac,
):
    rows, cols, width = cells.shape
    scale = 1.0 / math.sqrt(width)
    me_r = lax.axis_index("row")
    me_c = lax.axis_index("col")
    n_chunk = rows // chunk
    per = cols // n_row
    m_per = width // n_row
    q_rows = cols // 128

    def local(hbm, vmem, sem, k):
        return pltpu.make_async_copy(
            hbm.at[pl.ds(k * chunk, chunk)], vmem.at[pl.ds(k * chunk, chunk)], sem.at[k]
        )

    for k in range(n_chunk):
        local(up_hbm, up, up_sem, k).start()
    small_in = [
        pltpu.make_async_copy(src, dst, in_sem.at[i])
        for i, (src, dst) in enumerate(
            ((wk_hbm, wk_ref), (wv_hbm, wv_ref), (wo_hbm, wo_ref), (rq_hbm, rq_ref), (cq_hbm, cq_ref))
        )
    ]
    for copy in small_in:
        copy.start()
    for k in range(n_chunk):
        local(cells_hbm, cells, cell_sem, k).start()
    sub16 = lax.broadcasted_iota(jnp.int32, (16, 2 * width), 0)

    barrier = pltpu.get_barrier_semaphore()

    @pl.loop(1, n_row)
    def _(d):
        pl.semaphore_signal(
            barrier, inc=1, device_id=(lax.rem(me_r + d, n_row), me_c), device_id_type=MESH
        )

    @pl.loop(1, n_col)
    def _(d):
        pl.semaphore_signal(
            barrier, inc=1, device_id=(me_r, lax.rem(me_c + d, n_col)), device_id_type=MESH
        )

    def to_rows(src_of, dst, s_sem, r_sem, d):
        peer = lax.rem(me_r + d, n_row)
        return pltpu.make_async_remote_copy(
            src_ref=src_of(peer), dst_ref=dst.at[me_r], send_sem=s_sem.at[d],
            recv_sem=r_sem.at[d], device_id=(peer, me_c), device_id_type=MESH,
        )

    def from_rows(src_of, dst, s_sem, r_sem, d):
        peer = lax.rem(me_r + n_row - d, n_row)
        return pltpu.make_async_remote_copy(
            src_ref=src_of(peer), dst_ref=dst.at[peer], send_sem=s_sem.at[d],
            recv_sem=r_sem.at[d], device_id=(peer, me_c), device_id_type=MESH,
        )

    def to_cols(src, dst, s_sem, r_sem, d):
        peer = lax.rem(me_c + d, n_col)
        return pltpu.make_async_remote_copy(
            src_ref=src, dst_ref=dst.at[me_c], send_sem=s_sem.at[d],
            recv_sem=r_sem.at[d], device_id=(me_r, peer), device_id_type=MESH,
        )

    def from_cols(src, dst, s_sem, r_sem, d):
        peer = lax.rem(me_c + n_col - d, n_col)
        return pltpu.make_async_remote_copy(
            src_ref=src, dst_ref=dst.at[peer], send_sem=s_sem.at[d],
            recv_sem=r_sem.at[d], device_id=(me_r, peer), device_id_type=MESH,
        )

    half_n = n_row // 2
    me_core, me_chip = lax.rem(me_r, 2), lax.div(me_r, 2)
    mine, other = me_core * half_n, (1 - me_core) * half_n

    def to_sibling(src, dst, s_sem, r_sem):
        return pltpu.make_async_remote_copy(
            src_ref=src, dst_ref=dst, send_sem=s_sem, recv_sem=r_sem,
            device_id=(me_r + 1 - 2 * me_core, me_c), device_id_type=MESH,
        )

    def to_chips(src_of, dst, s_sem, r_sem, d):
        chip = lax.rem(me_chip + d, half_n)
        return pltpu.make_async_remote_copy(
            src_ref=src_of(chip), dst_ref=dst, send_sem=s_sem.at[d], recv_sem=r_sem.at[d],
            device_id=(chip * 2 + me_core, me_c), device_id_type=MESH,
        )

    def from_chips(dst_of, s_sem, r_sem, d):
        chip = lax.rem(me_chip + half_n - d, half_n)
        return pltpu.make_async_remote_copy(
            src_ref=dst_of(chip), dst_ref=dst_of(chip), send_sem=s_sem.at[d],
            recv_sem=r_sem.at[d], device_id=(chip * 2 + me_core, me_c), device_id_type=MESH,
        )

    def start_rows(*args):
        @pl.loop(1, n_row)
        def _(d):
            to_rows(*args, d).start()

    def wait_rows(*args):
        @pl.loop(1, n_row)
        def _(d):
            to_rows(*args, d).wait_send()
            from_rows(*args, d).wait_recv()

    def start_cols(*args):
        @pl.loop(1, n_col)
        def _(d):
            to_cols(*args, d).start()

    def wait_cols(*args):
        @pl.loop(1, n_col)
        def _(d):
            to_cols(*args, d).wait_send()
            from_cols(*args, d).wait_recv()

    span = 64
    groups = span // per
    for k in range(n_chunk):
        local(up_hbm, up, up_sem, k).wait()

        def add_block(cb, total, k=k):
            x = up[pl.ds(k * chunk, chunk), pl.ds(pl.multiple_of(cb * span, span), span), :]
            x = x.astype(F32)
            by_col = jnp.sum(x, 0).reshape(groups, per, width)
            at = pl.ds(cb * groups, groups)
            cot_loc[at] = by_col if k == 0 else cot_loc[at] + by_col
            return total + jnp.sum(x, 1)

        row_cot[pl.ds(k * chunk, chunk), :] = lax.fori_loop(
            0, cols // span, add_block, jnp.zeros((chunk, width), F32), unroll=2
        )

    pl.semaphore_wait(barrier, n_row + n_col - 2)
    swap = to_sibling(cot_loc.at[pl.ds(other, half_n)], pair_buf, s_pr.at[0], r_pr.at[0])
    swap.start()

    for copy in small_in:
        copy.wait()
    wk = wk_ref[...].astype(F32)
    queries = jnp.concatenate([rq_ref[...], cq_ref[...], jnp.zeros((6, width), F32)], 0)
    kvec = dot_nt(queries, wk, HIGH) * scale
    kr, kc = kvec[0:1], kvec[1:2]
    k_pieces = stack_rows(split(kr, 3) + split(kc, 3), width)
    ids = me_c * cols + lax.broadcasted_iota(jnp.int32, (1, cols), 1)

    swap.wait()
    chip_sum[...] = cot_loc[pl.ds(mine, half_n)] + pair_buf[...]
    rs_buf[me_chip] = chip_sum[me_chip]

    @pl.loop(1, half_n)
    def _(d):
        to_chips(lambda chip: chip_sum.at[chip], rs_buf.at[me_chip], s_rs, r_rs, d).start()

    @pl.loop(0, n_chunk)
    def _(k):
        local(cells_hbm, cells, cell_sem, k).wait()
        at = pl.ds(pl.multiple_of(k * chunk, chunk), chunk)
        s = dot_nt(k_pieces, cells[at].reshape(chunk * cols, width))
        one, two = [], []
        for i in range(chunk):
            x = s[:, i * cols : (i + 1) * cols]
            live = ids < counts[k * chunk + i]
            one.append(jnp.where(live, x[0:1] + x[1:2] + x[2:3], NEG_FILL))
            two.append(jnp.where(live, x[3:4] + x[4:5] + x[5:6], NEG_FILL))
        sr[at, :] = jnp.concatenate(one, 0)
        sc[at, :] = jnp.concatenate(two, 0)

    @pl.loop(1, half_n)
    def _(d):
        to_chips(lambda chip: chip_sum.at[chip], rs_buf.at[me_chip], s_rs, r_rs, d).wait_send()
        from_chips(lambda chip: rs_buf.at[chip], s_rs, r_rs, d).wait_recv()

    own = rs_buf[0]
    for i in range(1, half_n):
        own = own + rs_buf[i]
    cot_full[mine + me_chip] = own
    own_slot = cot_full.at[mine + me_chip]

    @pl.loop(1, half_n)
    def _(d):
        to_chips(lambda chip: own_slot, own_slot, s_ag, r_ag, d).start()


    score = sc[...]
    col_m = jnp.max(score, 0, keepdims=True)
    weight = jnp.where(score > 0.5 * NEG_FILL, jnp.exp(score - col_m), 0.0)
    wc[...] = weight
    col_t = jnp.sum(weight, 0, keepdims=True)
    for j, value in enumerate((col_m, col_t)):
        for i in range(q_rows):
            small[me_r, pl.ds(j * q_rows + i, 1), :] = value[:, i * 128 : (i + 1) * 128]
    small_x = (lambda peer: small.at[me_r], small, s_sm, r_sm)
    start_rows(*small_x)

    score = sr[...]
    row_m = jnp.max(score, 1, keepdims=True)
    row_weight = jnp.where(score > 0.5 * NEG_FILL, jnp.exp(score - row_m), 0.0)
    wr[...] = row_weight
    row_t = jnp.sum(row_weight, 1, keepdims=True)
    sub = lax.broadcasted_iota(jnp.int32, (chunk, 1), 0)

    @pl.loop(0, n_chunk)
    def _(k):
        at = pl.ds(pl.multiple_of(k * chunk, chunk), chunk)
        pieces = jnp.concatenate(split(wr[at, :], 2), 0).astype(BF16)
        acc = jnp.zeros((chunk, width), F32)
        for i in range(chunk):
            s = jnp.dot(pieces, cells[k * chunk + i], preferred_element_type=F32)
            acc = jnp.where(sub == i, s[0:chunk] + s[chunk : 2 * chunk], acc)
        row_pool[at, :] = acc

    row_buf[me_c, 0] = row_pool[...]
    row_buf[me_c, 1] = row_cot[...]
    row_buf[me_c, 2] = jnp.broadcast_to(row_m, (rows, width))
    row_buf[me_c, 3] = jnp.broadcast_to(row_t, (rows, width))
    row_x = (row_buf.at[me_c], row_buf, s_rx, r_rx)
    start_cols(*row_x)

    wait_cols(*row_x)
    top = row_buf[0, 2]
    for i in range(1, n_col):
        top = jnp.maximum(top, row_buf[i, 2])
    pool = jnp.zeros((rows, width), F32)
    total = jnp.zeros((rows, width), F32)
    cot = jnp.zeros((rows, width), F32)
    for i in range(n_col):
        decay = jnp.exp(row_buf[i, 2] - top)
        pool = pool + row_buf[i, 0] * decay
        total = total + row_buf[i, 3] * decay
        cot = cot + row_buf[i, 1]
    factor = jnp.exp(row_buf[me_c, 2] - top) / total
    both = jnp.dot(wv_ref[...], wo_ref[...], preferred_element_type=F32)
    g_row = dot_nt(cot, both, HIGH)
    row_grad[...] = g_row
    row_dot = jnp.sum(pool * g_row, 1, keepdims=True) / total[:, 0:1]
    row_prob = wr[...] * factor[:, 0:1]

    @pl.loop(1, half_n)
    def _(d):
        to_chips(lambda chip: own_slot, own_slot, s_ag, r_ag, d).wait_send()
        from_chips(lambda chip: cot_full.at[mine + chip], s_ag, r_ag, d).wait_recv()

    half_at = cot_full.at[pl.ds(mine, half_n)]
    fill = to_sibling(half_at, half_at, s_pr.at[1], r_pr.at[1])
    fill.start()

    @pl.loop(0, n_chunk)
    def _(k):
        at = pl.ds(pl.multiple_of(k * chunk, chunk), chunk)
        pieces = jnp.concatenate(split(row_grad[at, :], 2), 0).astype(BF16)
        acc = jnp.zeros((chunk, cols), F32)
        for i in range(chunk):
            s = dot_nt(pieces, cells[k * chunk + i])
            acc = jnp.where(sub == i, s[0:chunk] + s[chunk : 2 * chunk], acc)
        rdp[at, :] = acc

    row_ds = row_prob * (rdp[...] - row_dot)
    sr[...] = row_ds

    wait_rows(*small_x)
    top = small[0, 0:q_rows]
    for i in range(1, n_row):
        top = jnp.maximum(top, small[i, 0:q_rows])
    total = jnp.zeros((q_rows, 128), F32)
    for i in range(n_row):
        total = total + small[i, q_rows : 2 * q_rows] * jnp.exp(small[i, 0:q_rows] - top)
    f_col = jnp.exp(col_m - flat_row(top)) / flat_row(total)
    col_prob = wc[...] * f_col
    wc[...] = col_prob
    f_t = jnp.broadcast_to(f_col, (8, cols)).T[:, 0:1]

    fill.wait_send()
    other_at = cot_full.at[pl.ds(other, half_n)]
    to_sibling(other_at, other_at, s_pr.at[1], r_pr.at[1]).wait_recv()
    cot_all = cot_full[...].reshape(cols, width)
    g_col = dot_nt(cot_all, both, HIGH)
    g_out[...] = g_col

    @pl.loop(0, n_chunk)
    def _(k):
        at = pl.ds(pl.multiple_of(k * chunk, chunk), chunk)
        acc = jnp.zeros((16, cols), F32)
        for i in range(chunk):
            prod = cells[k * chunk + i].astype(F32) * g_out[...]
            hi = prod.astype(BF16)
            lo = (prod - hi.astype(F32)).astype(BF16)
            ones = jnp.where(sub16 == i, 1.0, 0.0).astype(BF16)
            acc = acc + dot_nt(ones, jnp.concatenate([hi, lo], 1))
        cdp[at, :] = acc[0:chunk]

    part_dot = jnp.sum(wc[...] * cdp[...], 0, keepdims=True)
    for i in range(q_rows):
        dots_buf[me_r, pl.ds(i, 1), :] = part_dot[:, i * 128 : (i + 1) * 128]
    dots_x = (lambda peer: dots_buf.at[me_r], dots_buf, s_dt, r_dt)
    start_rows(*dots_x)

    w_t = jnp.concatenate([p.T for p in split(weight, 2)], 1).astype(BF16)
    pick = lax.rem(lax.broadcasted_iota(jnp.int32, (2 * rows, 2 * width), 0), rows)
    lane = lax.broadcasted_iota(jnp.int32, (2 * rows, 2 * width), 1)
    pick = pick - jnp.where(lane < width, 0, 1)
    col_pool[...] = jnp.zeros_like(col_pool)

    @pl.loop(0, rows // 4)
    def _(k):
        acc = col_pool[...]
        for i in (0, 2):
            r = k * 4 + i
            one = jnp.where(pick == r, 1.0, 0.0).astype(BF16)
            spread = jnp.dot(w_t, one, preferred_element_type=F32)
            acc = acc + spread[:, :width] * cells[r].astype(F32)
            acc = acc + spread[:, width:] * cells[r + 1].astype(F32)
        col_pool[...] = acc

    m_loc = dot_tn(col_pool[...] * f_t, cot_all, HIGH)
    m_loc = m_loc + dot_tn(row_pool[...] * factor, cot, HIGH)
    for i in range(n_row):
        red_src[i, 0:m_per] = m_loc[i * m_per : (i + 1) * m_per]
        if m_per < 8:
            red_src[i, m_per:8] = jnp.zeros((8 - m_per, width), F32)
    reduce = (lambda peer: red_src.at[peer], red_buf, s_rd, r_rd)
    start_rows(*reduce)
    red_buf[me_r] = red_src[me_r]

    zero = jnp.zeros((rows, width), F32)
    one = jnp.ones((rows, width), F32)
    left = jnp.concatenate(
        [g_row, jnp.broadcast_to(kr, (rows, width)), jnp.broadcast_to(kc, (rows, width)), zero], 0
    )
    right = jnp.concatenate([zero, zero, zero, one], 0)
    half = jnp.concatenate([left, right], 1)
    base_out[...] = jnp.concatenate([half, half], 0)

    wait_rows(*dots_x)
    dots = dots_buf[0, 0:q_rows]
    for i in range(1, n_row):
        dots = dots + dots_buf[i, 0:q_rows]
    col_ds = wc[...] * (cdp[...] - flat_row(dots))
    sc[...] = col_ds

    turn = lax.rem(lax.broadcasted_iota(jnp.int32, (4 * chunk, 1), 0), chunk)

    def moments(k, acc):
        at = pl.ds(pl.multiple_of(k * chunk, chunk), chunk)
        pieces = split(sr[at, :], 2) + split(sc[at, :], 2)
        pieces = jnp.concatenate(pieces, 0).astype(BF16)
        for i in range(chunk):
            s = jnp.dot(pieces, cells[k * chunk + i], preferred_element_type=F32)
            acc = acc + jnp.where(turn == i, s, 0.0)
        return acc

    acc = lax.fori_loop(0, n_chunk, moments, jnp.zeros((4 * chunk, width), F32))
    ab_buf[me_r] = jnp.concatenate(
        [
            jnp.sum(acc[0 : 2 * chunk], 0, keepdims=True),
            jnp.sum(acc[2 * chunk : 4 * chunk], 0, keepdims=True),
            jnp.zeros((6, width), F32),
        ],
        0,
    )
    ab_x = (lambda peer: ab_buf.at[me_r], ab_buf, s_ab, r_ab)
    start_rows(*ab_x)

    wait_rows(*reduce)
    acc = red_buf[0]
    for i in range(1, n_row):
        acc = acc + red_buf[i]
    part[me_c] = acc
    col_x = (part.at[me_c], part, s_cx, r_cx)
    start_cols(*col_x)

    pieces = [split(x, 2) for x in (row_prob, row_ds, col_ds, wc[...])]
    for half in range(2):
        block = jnp.concatenate([p[half] for p in pieces], 0)
        lhs_out[:, half * 4 * rows : (half + 1) * 4 * rows] = block.T.astype(BF16)
    owner = lax.rem(lax.broadcasted_iota(jnp.int32, base_out.shape, 0), rows)

    def write(k):
        at = pl.ds(k * chunk, chunk)
        return pltpu.make_async_copy(up.at[at], raw_hbm.at[at], out_sem.at[k])

    def cell_grads(first, last):
        @pl.loop(first, last)
        def _(k):
            for i in range(chunk):
                r = k * chunk + i
                rhs = jnp.where(owner == r, base_out[...], 0.0).astype(BF16)
                res = jnp.dot(lhs_out[...], rhs, preferred_element_type=F32)
                delta = res[:, :width] + res[:, width:] * g_out[...]
                up[r] = (up[r].astype(F32) + delta).astype(BF16)
            write(k).start()

    cell_grads(0, n_chunk // 4)
    wait_cols(*col_x)
    acc = part[0]
    for i in range(1, n_col):
        acc = acc + part[i]
    m_full[me_r] = acc
    collect = (lambda peer: m_full.at[me_r], m_full, s_mg, r_mg)
    start_rows(*collect)
    cell_grads(n_chunk // 4, n_chunk // 2)

    wait_rows(*ab_x)
    acc = ab_buf[0]
    for i in range(1, n_row):
        acc = acc + ab_buf[i]
    ab_part[me_c] = acc
    ab_cx = (ab_part.at[me_c], ab_part, s_ac, r_ac)
    start_cols(*ab_cx)
    cell_grads(n_chunk // 2, n_chunk)
    wait_rows(*collect)
    m_out[...] = jnp.concatenate([m_full[i, 0:m_per] for i in range(n_row)], 0)
    wait_cols(*ab_cx)
    acc = ab_part[0]
    for i in range(1, n_col):
        acc = acc + ab_part[i]
    ab_out[...] = acc
    for k in range(n_chunk):
        write(k).wait()


def finish_kernel(
    pieces, raw_hbm, m_hbm, ab_hbm, wk_hbm, wv_hbm, wo_hbm, rq_hbm, cq_hbm,
    out_hbm, kwg_hbm, vwg_hbm, owg_hbm, rqg_hbm, cqg_hbm,
    stage, m_ref, ab_ref, wk_ref, wv_ref, wo_ref, rq_ref, cq_ref,
    kwg_ref, vwg_ref, owg_ref, rqg_ref, cqg_ref, in_sem, out_sem, arg_sem, res_sem,
):
    size = raw_hbm.shape[0] // pieces
    width = m_ref.shape[0]
    scale = 1.0 / math.sqrt(width)

    def copies(sources, targets, sem):
        return [
            pltpu.make_async_copy(src, dst, sem.at[i])
            for i, (src, dst) in enumerate(zip(sources, targets))
        ]

    arguments = copies(
        (m_hbm, ab_hbm, wk_hbm, wv_hbm, wo_hbm, rq_hbm, cq_hbm),
        (m_ref, ab_ref, wk_ref, wv_ref, wo_ref, rq_ref, cq_ref),
        arg_sem,
    )
    results = copies(
        (kwg_ref, vwg_ref, owg_ref, rqg_ref, cqg_ref),
        (kwg_hbm, vwg_hbm, owg_hbm, rqg_hbm, cqg_hbm),
        res_sem,
    )
    parts = [pl.ds(i * size, size) for i in range(pieces)]
    loads = copies([raw_hbm.at[p] for p in parts], [stage.at[p] for p in parts], in_sem)
    stores = copies([stage.at[p] for p in parts], [out_hbm.at[p] for p in parts], out_sem)
    for copy in arguments + loads:
        copy.start()

    def forward(first, last):
        for i in range(first, last):
            loads[i].wait()
            stores[i].start()

    for copy in arguments:
        copy.wait()
    forward(0, pieces // 4)
    ab, m = ab_ref[...], m_ref[...]
    queries = jnp.concatenate([rq_ref[...], cq_ref[...], jnp.zeros((6, width), F32)], 0)
    kwg_ref[...] = dot_tn(ab, queries * scale, HIGH)
    q_grad = dot_nn(ab, wk_ref[...].astype(F32), HIGH) * scale
    rqg_ref[...] = q_grad[0:1]
    cqg_ref[...] = q_grad[1:2]
    forward(pieces // 4, pieces // 2)
    vwg_ref[...] = dot_nt(m, wo_ref[...].astype(F32), HIGH)
    forward(pieces // 2, pieces)
    owg_ref[...] = dot_tn(wv_ref[...].astype(F32), m, HIGH)
    for copy in results:
        copy.start()
    for copy in stores + results:
        copy.wait()


def on_device(n_row, n_col, cells, upstream, counts, wk, wv, wo, rq, cq):
    rows, cols, width = cells.shape
    chunk = 8
    per = cols // n_row
    rq, cq = rq.reshape(1, width), cq.reshape(1, width)
    vmem = pl.BlockSpec(memory_space=pltpu.VMEM)
    hbm = pl.BlockSpec(memory_space=pl.ANY)
    n_chunk = rows // chunk
    dma = pltpu.SemaphoreType.DMA
    f32 = lambda *shape: pltpu.VMEM(shape, F32)
    small_rows = -(-2 * (cols // 128) // 8) * 8
    dots_rows = -(-(cols // 128) // 8) * 8
    square = jax.ShapeDtypeStruct((width, width), F32)
    vector = jax.ShapeDtypeStruct((1, width), F32)
    half_n = n_row // 2
    over_row, over_col, over_chip = dma((n_row,)), dma((n_col,)), dma((half_n,))
    raw, m, ab = pl.pallas_call(
        functools.partial(stats_kernel, n_row, n_col, chunk),
        out_shape=(
            jax.ShapeDtypeStruct(cells.shape, BF16),
            square,
            jax.ShapeDtypeStruct((8, width), F32),
        ),
        in_specs=[hbm, hbm, pl.BlockSpec(memory_space=pltpu.SMEM)] + [hbm] * 5,
        out_specs=(hbm, vmem, vmem),
        scratch_shapes=[
            pltpu.VMEM((cols, 8 * rows), BF16), f32(8 * rows, 2 * width), f32(cols, width),
            pltpu.VMEM(cells.shape, BF16), pltpu.VMEM(cells.shape, BF16),
            f32(n_row, per, width), f32(half_n, per, width), f32(half_n, per, width),
            f32(half_n, per, width), f32(n_row, per, width),
            f32(rows, width),
            f32(rows, cols), f32(rows, cols), f32(rows, cols), f32(rows, cols),
            f32(rows, cols), f32(rows, cols),
            f32(rows, width), f32(rows, width), f32(cols, width),
            f32(n_col, 4, rows, width),
            f32(n_row, small_rows, 128), f32(n_row, dots_rows, 128),
            f32(n_row, 8, width), f32(n_row, 8, width), f32(n_col, 8, width),
            f32(n_row, 8, width),
            f32(n_row, 8, width), f32(n_col, 8, width),
            pltpu.VMEM(wk.shape, BF16), pltpu.VMEM(wv.shape, BF16), pltpu.VMEM(wo.shape, BF16),
            f32(1, width), f32(1, width),
            dma((n_chunk,)), dma((n_chunk,)), dma((5,)), dma((n_chunk,)),
            dma((2,)), dma((2,)),
            over_chip, over_chip, over_chip, over_chip,
            over_col, over_col, over_row, over_row, over_row, over_row,
            over_row, over_row, over_col, over_col, over_row, over_row,
            over_row, over_row, over_col, over_col,
        ],
        compiler_params=pltpu.CompilerParams(
            collective_id=0, has_side_effects=True, vmem_limit_bytes=VMEM_BYTES
        ),
        name="hub_stats",
    )(cells, upstream, counts, wk, wv, wo, rq, cq)
    pieces = 8
    cell_grad, kwg, vwg, owg, rqg, cqg = pl.pallas_call(
        functools.partial(finish_kernel, pieces),
        out_shape=(
            jax.ShapeDtypeStruct(cells.shape, cells.dtype),
            square, square, square, vector, vector,
        ),
        in_specs=[hbm] * 8,
        out_specs=(hbm,) * 6,
        scratch_shapes=[
            pltpu.VMEM(cells.shape, BF16), f32(width, width), f32(8, width),
            pltpu.VMEM(wk.shape, BF16), pltpu.VMEM(wv.shape, BF16), pltpu.VMEM(wo.shape, BF16),
            f32(1, width), f32(1, width),
            f32(width, width), f32(width, width), f32(width, width), f32(1, width), f32(1, width),
            dma((pieces,)), dma((pieces,)), dma((7,)), dma((5,)),
        ],
        compiler_params=pltpu.CompilerParams(vmem_limit_bytes=VMEM_BYTES),
        name="finish",
    )(raw, m, ab, wk, wv, wo, rq, cq)
    return cell_grad, kwg, vwg, owg, rqg.reshape(width), cqg.reshape(width)


def solution(mesh):
    placed = (P("row", "col", None), P("row", "col", None), P("row"), P(), P(), P(), P(), P())
    return jax.shard_map(
        functools.partial(on_device, mesh.shape["row"], mesh.shape["col"]),
        mesh=mesh,
        in_specs=placed,
        out_specs=(P("row", "col", None), P(), P(), P(), P(), P()),
        check_vma=False,
    )
```
